512 devices in a mesh: lon: 32 (over y_lo, z), lat: 16 (over x, y_hi, core).
Axes of the slice: x: 4, y: 4 (y_hi: 2, y_lo: 2; y = y_hi * 2 + y_lo), z: 16, core: 2. Of those that a mesh axis runs over, the one named last changes fastest.
Arguments:
- grid_in: bfloat16 [128, 1024, 256], P('lat', 'lon'), may hold values from -6 to 6
- basis: bfloat16 [128, 3, 17, 4], replicated, may hold values from -3 to 3
- widths: int32 [128], replicated, may hold values from 1 to 8, as said below
- weight_one: bfloat16 [4, 256, 256], replicated, may hold values from -0.1875 to 0.1875
- weight_two: bfloat16 [4, 256, 256], replicated, may hold values from -0.1875 to 0.1875
- cotangent: bfloat16 [128, 1024, 256], P('lat', 'lon'), may hold values from -6 to 6
Outputs:
- grad_input: float32 [128, 1024, 256], P('lat', 'lon')
- grad_one: float32 [4, 256, 256], replicated
- grad_two: float32 [4, 256, 256], replicated
The draws below stay inside these ranges and needn't reach their ends.
Inputs may be any that keep to these rules, and one draw needn't show every extreme that they name: `widths`: both pole rows (row 0 and row 127) have width 8.
All inputs are finite; a program needn't handle non-finite values.
Results may differ from the reference program's by a relative error of at most 0.0067.
Values may be sent and summed in bfloat16 or wider, within the bound.
A program may use at most 64 MiB of HBM per device.

```python
import jax
import jax.numpy as jnp
from jax import lax

CHANNELS = 256
BASIS = 4
REACH = 8
LAT_DEV = 8
LON_DEV = 32
NLAT = 128
NLON = 1024


def draw_widths(key, part):
    key = jax.random.fold_in(key, 11)
    row_index = jnp.arange(NLAT, dtype=jnp.int32)
    from_pole = jnp.minimum(row_index, NLAT - 1 - row_index)
    free_width = jax.random.randint(key, (NLAT,), 1, REACH + 1, dtype=jnp.int32)
    widen = jnp.minimum(REACH, REACH * LAT_DEV // (from_pole + LAT_DEV)) // 2
    inner = jnp.maximum(free_width, widen)
    return jnp.where(from_pole == 0, REACH, inner).astype(jnp.int32)


def block_levels(own_key, shape, cuts, smallest, top_value):
    gain, own = 1.0, jax.random.fold_in(own_key, 6)
    for axis_at, parts in cuts:
        steps = jnp.exp(jax.random.uniform(jax.random.fold_in(own, axis_at), (parts,), jnp.float32, smallest / len(cuts), top_value / len(cuts)))
        gain = gain * jnp.repeat(steps, shape[axis_at] // parts).reshape([-1 if axis == axis_at else 1 for axis in range(len(shape))])
    return gain


def scatter_about(stream_key, shape, spread, bound, pieces=(), held_as=jnp.bfloat16):
    gain = block_levels(stream_key, shape, pieces, -0.22, 0.18) if pieces else 1.0
    values = jax.random.normal(stream_key, shape, jnp.float32) * spread * gain
    return jnp.minimum(jnp.maximum(values, -bound), bound).astype(held_as)


def setup_inputs(seed: int = 0) -> dict:
    arg_keys = jax.random.split(jax.random.key(seed), 7)
    return {
        "grid_in": scatter_about(arg_keys[0], (NLAT, NLON, CHANNELS), 1.0, 6.0, ((0, 16), (1, 32))),
        "basis": scatter_about(arg_keys[1], (NLAT, 3, 2 * REACH + 1, BASIS), 0.5, 3.0),
        "widths": draw_widths(jax.random.fold_in(arg_keys[6], 71), 0),
        "weight_one": scatter_about(arg_keys[3], (BASIS, CHANNELS, CHANNELS), (BASIS * CHANNELS) ** -0.5, 0.1875),
        "weight_two": scatter_about(arg_keys[4], (BASIS, CHANNELS, CHANNELS), (BASIS * CHANNELS) ** -0.5, 0.1875),
        "cotangent": scatter_about(arg_keys[5], (NLAT, NLON, CHANNELS), 1.0, 6.0, ((0, 16), (1, 32))),
    }


GELU_C = 0.7978845608028654
CUBIC = 0.044715
HIGHEST_PREC = lax.Precision.HIGHEST


def gelu_value(pre_act):
    return 0.5 * pre_act * (1.0 + jnp.tanh(GELU_C * (pre_act + CUBIC * pre_act * pre_act * pre_act)))


def gelu_slope(pre_act):
    tanh_val = jnp.tanh(GELU_C * (pre_act + CUBIC * pre_act * pre_act * pre_act))
    return 0.5 * (1.0 + tanh_val) + 0.5 * pre_act * (1.0 - tanh_val * tanh_val) * GELU_C * (1.0 + 3.0 * CUBIC * pre_act * pre_act)


def masked_basis(basis, widths):
    span_size = basis.shape[2]
    reach_cols = (span_size - 1) // 2
    offsets = jnp.arange(span_size, dtype=jnp.int32) - reach_cols
    keep_mask = (jnp.abs(offsets)[None, :] <= widths[:, None]).astype(jnp.float32)
    return basis.astype(jnp.float32) * keep_mask[:, None, :, None]


def pole_basis(masked):
    blank_slot = jnp.zeros_like(masked[0, 0])
    north_row = jnp.stack([blank_slot, blank_slot, masked[0, 0]])
    south_row = jnp.stack([masked[-1, 2], blank_slot, blank_slot])
    return jnp.concatenate([north_row[None], masked, south_row[None]], axis=0)


def offset_table(col_count, span_size, flipped):
    col_out = jnp.arange(col_count, dtype=jnp.int32)[:, None, None]
    col_in = jnp.arange(col_count + span_size - 1, dtype=jnp.int32)[None, :, None]
    offset_idx = jnp.arange(span_size, dtype=jnp.int32)[None, None, :]
    if flipped:
        diff_index = col_out - col_in + span_size - 1
    else:
        diff_index = col_in - col_out
    return (diff_index == offset_idx).astype(jnp.float32)


def extend_full(values):
    top_row = jnp.roll(values[0], NLON // 2, axis=-2)
    bottom_row = jnp.roll(values[-1], NLON // 2, axis=-2)
    stacked = jnp.concatenate([top_row[None], values, bottom_row[None]], axis=0)
    return jnp.concatenate([stacked[..., NLON - REACH:, :], stacked, stacked[..., :LON_DEV - REACH, :]], axis=-2)


def windows(padded):
    lead_shape = padded.shape[:-2]
    chan_count = padded.shape[-1]
    blocks = NLON // LON_DEV
    main_cols = padded[..., :NLON, :].reshape(lead_shape + (blocks, LON_DEV, chan_count))
    after_cols = padded[..., LON_DEV:NLON + LON_DEV, :].reshape(lead_shape + (blocks, LON_DEV, chan_count))
    return jnp.concatenate([main_cols, after_cols[..., :2 * REACH, :]], axis=-2)


def convolve_rows(grid_ext, masked, forward_table):
    def one_row(row_index):
        three_rows = lax.dynamic_slice_in_dim(grid_ext, row_index, 3, 0)
        row_basis = lax.dynamic_slice_in_dim(masked, row_index, 1, 0)[0]
        band_matrix = jnp.einsum('rtk,jmt->rkjm', row_basis, forward_table, precision=HIGHEST_PREC)
        windowed = windows(three_rows).astype(jnp.float32)
        mixed = jnp.einsum('rkjm,rbmc->kbjc', band_matrix, windowed, precision=HIGHEST_PREC)
        return mixed.reshape(BASIS, NLON, CHANNELS).astype(jnp.bfloat16)
    return lax.map(one_row, jnp.arange(NLAT, dtype=jnp.int32))


def adjoint_rows(grad_ext, pole_ext, flipped_table):
    def one_row(row_index):
        three_rows = lax.dynamic_slice_in_dim(grad_ext, row_index, 3, 0)[::-1]
        three_basis = lax.dynamic_slice_in_dim(pole_ext, row_index, 3, 0)[::-1]
        chosen = jnp.stack([three_basis[0, 0], three_basis[1, 1], three_basis[2, 2]])
        band_matrix = jnp.einsum('rtk,jmt->rkjm', chosen, flipped_table, precision=HIGHEST_PREC)
        windowed = windows(three_rows).astype(jnp.float32)
        result = jnp.einsum('rkjm,rkbmc->bjc', band_matrix, windowed, precision=HIGHEST_PREC)
        return result.reshape(NLON, CHANNELS)
    return lax.map(one_row, jnp.arange(NLAT, dtype=jnp.int32))


def weights_back(acts, grads, weight):
    weight_f = weight.astype(jnp.float32)

    def step(grad_total, row_pair):
        act_row, grad_row = row_pair
        act_f = act_row.astype(jnp.float32)
        grad_f = grad_row.astype(jnp.float32)
        grad_total = grad_total + jnp.einsum('kjc,jo->kco', act_f, grad_f, precision=HIGHEST_PREC)
        row_grad = jnp.einsum('jo,kco->kjc', grad_f, weight_f, precision=HIGHEST_PREC).astype(jnp.bfloat16)
        return grad_total, row_grad
    return lax.scan(step, jnp.zeros((BASIS, CHANNELS, CHANNELS), jnp.float32), (acts, grads))


def reference(grid_in, basis, widths, weight_one, weight_two, cotangent):
    masked = masked_basis(basis, widths)
    pole_ext = pole_basis(masked)
    span_size = 2 * REACH + 1
    forward_table = offset_table(LON_DEV, span_size, False)
    flipped_table = offset_table(LON_DEV, span_size, True)
    weight_f = weight_one.astype(jnp.float32)

    def mix_row(act_row):
        pre_act = jnp.einsum('kjc,kco->jo', act_row.astype(jnp.float32), weight_f, precision=HIGHEST_PREC)
        return gelu_value(pre_act).astype(jnp.bfloat16), gelu_slope(pre_act)

    z_one = convolve_rows(extend_full(grid_in), masked, forward_table)
    hidden, slope = lax.map(mix_row, z_one)
    z_two = convolve_rows(extend_full(hidden), masked, forward_table)
    grad_two, dz_two = weights_back(z_two, cotangent, weight_two)
    grad_hidden = adjoint_rows(extend_full(dz_two), pole_ext, flipped_table)
    grad_act = (grad_hidden * slope).astype(jnp.bfloat16)
    grad_one, dz_one = weights_back(z_one, grad_act, weight_one)
    grad_input = adjoint_rows(extend_full(dz_one), pole_ext, flipped_table)
    return (grad_input, grad_one, grad_two)
```

```python
import functools

import jax
import jax.numpy as jnp
from jax import lax
from jax.experimental import pallas as pl
from jax.experimental.pallas import tpu as pltpu
from jax.sharding import PartitionSpec as P

GELU_C = 0.7978845608028654
CUBIC = 0.044715
MESH = pl.DeviceIdType.MESH

ROWS, COLS, CH, KB, REACH = 8, 32, 256, 4, 8
HALO = 2 * REACH
XR, XC = ROWS + 4, COLS + 2 * HALO
MR, MC = ROWS + 2, COLS + 2 * REACH
TAP = 3 * XC
HALF = KB * CH // 2


def dot(a, b):
    return jnp.dot(a, b, preferred_element_type=jnp.float32)


def dot_t(a, b):
    return lax.dot_general(a, b, (((1,), (1,)), ((), ())), preferred_element_type=jnp.float32)


def t_dot(a, b):
    return lax.dot_general(a, b, (((0,), (0,)), ((), ())), preferred_element_type=jnp.float32)


def loop(count, body):
    lax.fori_loop(0, count, lambda i, c: (body(i), c)[1], 0, unroll=True)


def kernel(
    nlat,
    nlon,
    grid_ref,
    tab_ref,
    w1_ref,
    w2_ref,
    cot_ref,
    gin_ref,
    out1_ref,
    out2_ref,
    gext,
    cext,
    fband,
    aband,
    w1,
    w2,
    zbuf,
    z1own,
    z2,
    slope,
    hid,
    gact,
    gown,
    part1,
    part2,
    crecv,
    xsend,
    xrecv,
    zown,
    zrecv,
    zall,
    local_sem,
    halo_send,
    halo_recv,
    core_send,
    core_recv,
    x_send,
    x_recv,
    z_send,
    z_recv,
    zg_send,
    zg_recv,
    xg_send,
    xg_recv,
    f_send,
    f_recv,
):
    nx, nz = nlat // 4, nlon // 2
    npl = nx * 4
    xr = HALF // npl
    zr = 2 * xr // nz
    zh = nz // 2
    lat, lon = lax.axis_index("lat"), lax.axis_index("lon")
    core = lat % 2
    z = lon % nz
    me = (lat // 2) * 2 + lon // nz

    def at(la, lo):
        return {"lat": la, "lon": lo}

    def in_plane(q):
        return at((q // 2) * 2 + core, (q % 2) * nz + z)

    def in_z(q):
        return at(lat, (lon // nz) * nz + q)

    north = (lat == 0).astype(jnp.int32)
    south = (lat == nlat - 1).astype(jnp.int32)
    turn = nlon // 2
    up = (lat - 1 + north, (lon + turn * north) % nlon)
    down = (lat + 1 - south, (lon + turn * south) % nlon)
    west, east = (lon + nlon - 1) % nlon, (lon + 1) % nlon
    sibling = at(lat + 1 - 2 * core, lon)

    def beside(place, step):
        return at(place[0], (place[1] + nlon + step) % nlon)

    up_row = (XR - 2) * (1 - north)
    down_row = (XR - 2) * south
    neighbours = [
        (at(lat, west), slice(0, ROWS), slice(0, HALO), 2, ROWS, COLS + HALO, HALO),
        (at(lat, east), slice(0, ROWS), slice(COLS - HALO, COLS), 2, ROWS, 0, HALO),
        (at(*up), slice(0, 2), slice(0, COLS), up_row, 2, HALO, COLS),
        (at(*down), slice(ROWS - 2, ROWS), slice(0, COLS), down_row, 2, HALO, COLS),
        (beside(up, -1), slice(0, 2), slice(0, HALO), up_row, 2, COLS + HALO, HALO),
        (beside(up, 1), slice(0, 2), slice(COLS - HALO, COLS), up_row, 2, 0, HALO),
        (beside(down, -1), slice(ROWS - 2, ROWS), slice(0, HALO), down_row, 2, COLS + HALO, HALO),
        (beside(down, 1), slice(ROWS - 2, ROWS), slice(COLS - HALO, COLS), down_row, 2, 0, HALO),
    ]

    own = (
        pltpu.make_async_copy(
            grid_ref, gext.at[pl.ds(2, ROWS), pl.ds(HALO, COLS)], local_sem.at[0]
        ),
        pltpu.make_async_copy(cot_ref, cext.at[pl.ds(2, ROWS), pl.ds(HALO, COLS)], local_sem.at[1]),
        pltpu.make_async_copy(w1_ref, w1, local_sem.at[2]),
        pltpu.make_async_copy(w2_ref, w2, local_sem.at[3]),
    )
    for copy in own:
        copy.start()

    barrier = pltpu.get_barrier_semaphore()

    def greet(device):
        pl.semaphore_signal(barrier, inc=1, device_id=device, device_id_type=MESH)

    for device, *_ in neighbours:
        greet(device)
    greet(sibling)
    loop(npl - 1, lambda i: greet(in_plane((me + 1 + i) % npl)))
    loop(nz - 1, lambda i: greet(in_z((z + 1 + i) % nz)))
    pl.semaphore_wait(barrier, len(neighbours) + 1 + npl - 1 + nz - 1)

    for which, (src, ext) in enumerate(((grid_ref, gext), (cot_ref, cext))):
        for device, rows, cols, row, count, col, width in neighbours:
            pltpu.make_async_remote_copy(
                src_ref=src.at[rows, cols],
                dst_ref=ext.at[pl.ds(row, count), pl.ds(col, width)],
                send_sem=halo_send.at[which],
                recv_sem=halo_recv.at[which],
                device_id=device,
                device_id_type=MESH,
            ).start()

    def await_bytes(ref, sem):
        pltpu.make_async_copy(ref, ref, sem).wait()

    def build(which, band):
        def one(v):
            for k in range(KB):
                for h in range(2):
                    taps = tab_ref[which, v, pl.ds(2 * k + h, 1), :]
                    taps = jnp.broadcast_to(taps, (MC, 128))
                    rolled = pltpu.roll(taps, 0, 1, stride=1, stride_axis=0)
                    band[v, k * MC : (k + 1) * MC, h * 128 : (h + 1) * 128] = rolled.astype(
                        jnp.bfloat16
                    )

        loop(MR, one)

    build(0, fband)
    build(1, aband)
    for buf in (hid, gact):
        buf[:, MC:XC, :] = jnp.zeros((MR, XC - MC, CH), jnp.bfloat16)

    def slot(v):
        if v < 2:
            return v + north * (1 - 2 * v)
        if v >= XR - 2:
            return v + south * (2 * (XR - 2) + 1 - 2 * v)
        return v

    def conv_wide(ext, band, keep_own):
        for v in range(MR):
            rows = jnp.concatenate([ext[slot(v + r)] for r in range(3)], axis=0)
            full = dot(band[v, :, :TAP], rows)
            mixed = full.astype(jnp.bfloat16)
            for k in range(KB):
                zbuf[v * MC : (v + 1) * MC, k * CH : (k + 1) * CH] = mixed[
                    k * MC : (k + 1) * MC, :
                ]
            if keep_own and 1 <= v <= ROWS:
                for k in range(KB):
                    z1own[k, (v - 1) * COLS : v * COLS, :] = full[
                        k * MC + REACH : k * MC + REACH + COLS, :
                    ].astype(jnp.bfloat16)

    def conv_own(src, band, store):
        for i in range(ROWS):
            taps = jnp.concatenate(
                [band[i + 1, k * MC : k * MC + COLS, :TAP] for k in range(KB)], axis=0
            )
            rows = src[i : i + 3].reshape(TAP, CH)
            mixed = dot(taps, rows).astype(jnp.bfloat16)
            for k in range(KB):
                store(i, k, mixed[k * COLS : (k + 1) * COLS, :])

    own[0].wait()
    await_bytes(gext.at[pl.ds(0, ROWS)], halo_recv.at[0])
    conv_wide(gext, fband, True)
    own[2].wait()
    act = dot(zbuf[...], w1[...].reshape(KB * CH, CH))
    tanh_val = jnp.tanh(GELU_C * (act + CUBIC * act * act * act))
    slope[...] = 0.5 * (1.0 + tanh_val) + 0.5 * act * (1.0 - tanh_val * tanh_val) * GELU_C * (
        1.0 + 3.0 * CUBIC * act * act
    )
    hidden = (0.5 * act * (1.0 + tanh_val)).astype(jnp.bfloat16)
    for v in range(MR):
        hid[v, :MC, :] = hidden[v * MC : (v + 1) * MC, :]

    def weight_grad(cells, grad, part, g):
        for step in range(KB):
            k = (2 * (1 - core) + step) % KB
            part[k] = t_dot(cells[k], grad)
            if step < 2:
                pltpu.make_async_remote_copy(
                    src_ref=part.at[k],
                    dst_ref=crecv.at[g, step],
                    send_sem=core_send.at[g],
                    recv_sem=core_recv.at[g],
                    device_id=sibling,
                    device_id_type=MESH,
                ).start()

    def store_z2(i, k, value):
        z2[k, i * COLS : (i + 1) * COLS, :] = value

    conv_own(hid, fband, store_z2)
    own[1].wait()
    weight_grad(z2, cext[2 : 2 + ROWS, HALO : HALO + COLS, :].reshape(ROWS * COLS, CH), part2, 1)

    def mix_back(cells, weight):
        total = dot_t(cells[:, :CH], weight[0])
        for k in range(1, KB):
            total = total + dot_t(cells[:, k * CH : (k + 1) * CH], weight[k])
        return total

    await_bytes(cext.at[pl.ds(0, ROWS)], halo_recv.at[1])
    conv_wide(cext, aband, False)
    own[3].wait()
    grad_act = mix_back(zbuf, w2) * slope[...]
    for v in range(MR):
        gact[v, :MC, :] = grad_act[v * MC : (v + 1) * MC, :].astype(jnp.bfloat16)
        if 1 <= v <= ROWS:
            gown[(v - 1) * COLS : v * COLS, :] = grad_act[
                v * MC + REACH : v * MC + REACH + COLS, :
            ].astype(jnp.bfloat16)
    weight_grad(z1own, gown[...], part1, 0)

    parts = (part1, part2)
    outs = (out1_ref, out2_ref)
    own_half = 2 * core

    def plane_chunk(g, q):
        k, row = q * xr // CH, (q * xr) % CH
        row = pl.multiple_of(row, xr)
        return parts[g][own_half + k, pl.ds(row, xr), :] + crecv[g, k, pl.ds(row, xr), :]

    def plane_scatter(g):
        await_bytes(crecv.at[g], core_recv.at[g])

        def one(i):
            q = (me + 1 + i) % npl
            xsend[g, i] = plane_chunk(g, q).astype(jnp.bfloat16)
            pltpu.make_async_remote_copy(
                src_ref=xsend.at[g, i],
                dst_ref=xrecv.at[g, i],
                send_sem=x_send.at[g],
                recv_sem=x_recv.at[g],
                device_id=in_plane(q),
                device_id_type=MESH,
            ).start()

        loop(npl - 1, one)

    def z_scatter(g):
        total = plane_chunk(g, me)
        await_bytes(xrecv.at[g], x_recv.at[g])
        for i in range(npl - 1):
            total = total + xrecv[g, i].astype(jnp.float32)
        for q in range(nz):
            zown[g, q] = total[
                (q % zh) * zr : (q % zh + 1) * zr, (q // zh) * 128 : (q // zh + 1) * 128
            ]

        def one(i):
            q = (z + 1 + i) % nz
            pltpu.make_async_remote_copy(
                src_ref=zown.at[g, q],
                dst_ref=zrecv.at[g, i],
                send_sem=z_send.at[g],
                recv_sem=z_recv.at[g],
                device_id=in_z(q),
                device_id_type=MESH,
            ).start()

        loop(nz - 1, one)

    def z_gather(g):
        total = zown[g, z]
        await_bytes(zrecv.at[g], z_recv.at[g])
        for i in range(nz - 1):
            total = total + zrecv[g, i]
        zall[g, z] = total

        def one(i):
            pltpu.make_async_remote_copy(
                src_ref=zall.at[g, z],
                dst_ref=zall.at[g, z],
                send_sem=zg_send.at[g],
                recv_sem=zg_recv.at[g],
                device_id=in_z((z + 1 + i) % nz),
                device_id_type=MESH,
            ).start()

        loop(nz - 1, one)

    def plane_gather(g):
        await_bytes(zall.at[g, pl.ds(0, nz - 1)], zg_recv.at[g])
        left = jnp.concatenate([zall[g, q] for q in range(zh)], axis=0)
        right = jnp.concatenate([zall[g, zh + q] for q in range(zh)], axis=0)
        rows = pl.ds(pl.multiple_of(core * HALF + me * xr, xr), xr)
        out = outs[g]
        out[rows, :] = jnp.concatenate([left, right], axis=1).astype(jnp.bfloat16)

        def one(i):
            pltpu.make_async_remote_copy(
                src_ref=out.at[rows],
                dst_ref=out.at[rows],
                send_sem=xg_send.at[g],
                recv_sem=xg_recv.at[g],
                device_id=in_plane((me + 1 + i) % npl),
                device_id_type=MESH,
            ).start()

        loop(npl - 1, one)

    def core_gather(g):
        out = outs[g]
        await_bytes(out.at[pl.ds(0, (npl - 1) * xr)], xg_recv.at[g])
        rows = pl.ds(pl.multiple_of(core * HALF, HALF), HALF)
        pltpu.make_async_remote_copy(
            src_ref=out.at[rows],
            dst_ref=out.at[rows],
            send_sem=f_send.at[g],
            recv_sem=f_recv.at[g],
            device_id=sibling,
            device_id_type=MESH,
        ).start()

    plane_scatter(1)
    plane_scatter(0)

    def store_back(i, k, value):
        zbuf[i * COLS : (i + 1) * COLS, k * CH : (k + 1) * CH] = value

    conv_own(gact, aband, store_back)
    gin_ref[...] = mix_back(zbuf.at[pl.ds(0, ROWS * COLS)], w1)

    z_scatter(1)
    z_scatter(0)
    z_gather(1)
    z_gather(0)
    plane_gather(1)
    plane_gather(0)
    core_gather(1)
    core_gather(0)
    for which, ext in enumerate((gext, cext)):
        await_bytes(ext.at[pl.ds(0, ROWS)], halo_send.at[which])
    for g in range(2):
        await_bytes(crecv.at[g], core_send.at[g])
        await_bytes(xrecv.at[g], x_send.at[g])
        await_bytes(zrecv.at[g], z_send.at[g])
        await_bytes(zall.at[g, pl.ds(0, nz - 1)], zg_send.at[g])
        await_bytes(outs[g].at[pl.ds(0, (npl - 1) * xr)], xg_send.at[g])
    for g in range(2):
        await_bytes(outs[g].at[pl.ds(0, HALF)], f_recv.at[g])
        await_bytes(outs[g].at[pl.ds(0, HALF)], f_send.at[g])


def tap_table(basis, widths):
    span = basis.shape[2]
    keep = jnp.abs(jnp.arange(span) - REACH)[None, :] <= widths[:, None]
    masked = jnp.where(keep[:, None, :, None], basis.astype(jnp.float32), 0.0)
    masked = jnp.concatenate([masked[1::-1, ::-1], masked, masked[:-3:-1, ::-1]], axis=0)
    rows = lax.dynamic_slice_in_dim(masked, lax.axis_index("lat") * ROWS, XR, 0)
    forward = rows[1 : 1 + MR]
    back = jnp.stack([rows[s : s + MR, 2 - s, ::-1] for s in range(3)], axis=1)
    both = jnp.stack([forward, back]).transpose(0, 1, 4, 2, 3)
    both = jnp.pad(both, ((0, 0), (0, 0), (0, 0), (0, 1), (0, XC - span)))
    return both.reshape(2, MR, 2 * KB, 128)


def local(grid_in, basis, widths, weight_one, weight_two, cotangent):
    nlat, nlon = lax.axis_size("lat"), lax.axis_size("lon")
    npl, nz = nlat, nlon // 2
    xr = HALF // npl
    zr = 2 * xr // nz
    bf16, f32 = jnp.bfloat16, jnp.float32
    vmem, dma = pltpu.VMEM, pltpu.SemaphoreType.DMA
    hbm = pl.BlockSpec(memory_space=pl.ANY)
    on_chip = pl.BlockSpec(memory_space=pltpu.VMEM)
    grad_in, one, two = pl.pallas_call(
        functools.partial(kernel, nlat, nlon),
        out_shape=(
            jax.ShapeDtypeStruct((ROWS * COLS, CH), f32),
            jax.ShapeDtypeStruct((KB * CH, CH), bf16),
            jax.ShapeDtypeStruct((KB * CH, CH), bf16),
        ),
        in_specs=[hbm, on_chip, hbm, hbm, hbm],
        out_specs=(on_chip, on_chip, on_chip),
        scratch_shapes=[
            vmem((XR, XC, CH), bf16),
            vmem((XR, XC, CH), bf16),
            vmem((MR, KB * MC, 256), bf16),
            vmem((MR, KB * MC, 256), bf16),
            vmem((KB, CH, CH), bf16),
            vmem((KB, CH, CH), bf16),
            vmem((MR * MC, KB * CH), bf16),
            vmem((KB, ROWS * COLS, CH), bf16),
            vmem((KB, ROWS * COLS, CH), bf16),
            vmem((MR * MC, CH), f32),
            vmem((MR, XC, CH), bf16),
            vmem((MR, XC, CH), bf16),
            vmem((ROWS * COLS, CH), bf16),
            vmem((KB, CH, CH), f32),
            vmem((KB, CH, CH), f32),
            vmem((2, 2, CH, CH), f32),
            vmem((2, npl - 1, xr, CH), bf16),
            vmem((2, npl - 1, xr, CH), bf16),
            vmem((2, nz, zr, 128), f32),
            vmem((2, nz - 1, zr, 128), f32),
            vmem((2, nz, zr, 128), f32),
            dma((4,)),
        ]
        + [dma((2,))] * 14,
        compiler_params=pltpu.CompilerParams(
            collective_id=0, has_side_effects=True, vmem_limit_bytes=48 * 1024 * 1024
        ),
    )(grid_in, tap_table(basis, widths), weight_one, weight_two, cotangent)
    shape = weight_one.shape
    return (
        grad_in.reshape(grid_in.shape),
        one.astype(f32).reshape(shape),
        two.astype(f32).reshape(shape),
    )


def solution(mesh):
    placed = (P("lat", "lon", None), P(), P(), P(), P(), P("lat", "lon", None))
    return jax.shard_map(
        local,
        mesh=mesh,
        in_specs=placed,
        out_specs=(P("lat", "lon", None), P(), P()),
        check_vma=False,
    )
```

```python
import functools

import jax
import jax.numpy as jnp
from jax import lax
from jax.experimental import pallas as pl
from jax.experimental.pallas import tpu as pltpu
from jax.sharding import PartitionSpec as P

GELU_C = 0.7978845608028654
CUBIC = 0.044715
MESH = pl.DeviceIdType.MESH

ROWS, COLS, CH, KB, REACH = 8, 32, 256, 4, 8
HALO = 2 * REACH
XR, XC = ROWS + 4, COLS + 2 * HALO
MR, MC = ROWS + 2, COLS + 2 * REACH
TAP = 3 * XC
SPAN = 2 * REACH + 1
TAPS = 64
SLOT = 16
HALF = KB * CH // 2


def dot(a, b):
    return jnp.dot(a, b, preferred_element_type=jnp.float32)


def dot_t(a, b):
    return lax.dot_general(a, b, (((1,), (1,)), ((), ())), preferred_element_type=jnp.float32)


def t_dot(a, b):
    return lax.dot_general(a, b, (((0,), (0,)), ((), ())), preferred_element_type=jnp.float32)


def loop(count, body):
    lax.fori_loop(0, count, lambda i, c: (body(i), c)[1], 0, unroll=True)


def ring_steps(count):
    return sorted(range(1, count), key=lambda d: -min(d, count - d))


def plane_steps(nx, ny):
    steps = [(dx, dy) for dx in range(nx) for dy in range(ny) if dx or dy]
    return sorted(steps, key=lambda s: -min(s[0], nx - s[0]) - min(s[1], ny - s[1]))


def iota(rows, cols, axis):
    return lax.broadcasted_iota(jnp.int32, (rows, cols), axis)


def one_hot(where):
    return where.astype(jnp.float32).astype(jnp.bfloat16)


def spread_taps(basis_ref, widths_ref, taps, tab, lat, nlat_all):
    zeros = jnp.zeros((KB * TAPS, nlat_all), jnp.float32)
    taps[0], taps[1] = zeros, zeros
    widths = widths_ref[...]
    for r in range(3):
        for s in range(SPAN):
            block = basis_ref[r * SPAN + s].astype(jnp.float32)
            block = jnp.where(widths >= abs(s - REACH), block, 0.0)
            taps[0, pl.ds(r * SPAN + s, KB, stride=TAPS), :] = block
            taps[1, pl.ds((2 - r) * SPAN + s, KB, stride=TAPS), :] = block
    picks = []
    for j in range(3):
        row = lat * ROWS - 2 + j + iota(SLOT, nlat_all, 0)
        past = (row < 0) | (row >= nlat_all)
        true_row = jnp.where(row < 0, -1 - row, jnp.where(past, 2 * nlat_all - 1 - row, row))
        hit = true_row == iota(SLOT, nlat_all, 1)
        picks.append((one_hot(hit & jnp.logical_not(past)), one_hot(hit & past)))
    plain = jnp.concatenate([p for p, _ in picks], axis=0)
    mirror = jnp.concatenate([m for _, m in picks], axis=0)
    found = []
    for k in range(KB):
        rows = slice(k * TAPS, (k + 1) * TAPS)
        found.append(
            dot_t(plain, taps[0, rows, :].astype(jnp.bfloat16))
            + dot_t(mirror, taps[1, rows, :].astype(jnp.bfloat16))
        )

    def of(j):
        parts = [f[j * SLOT : (j + 1) * SLOT, :] for f in found]
        return jnp.concatenate(parts, axis=0).astype(jnp.bfloat16)

    source, lane = iota(TAPS, 4 * XC, 0), iota(TAPS, 4 * XC, 1)
    r, s = lane // XC, lane % XC
    used = (s < SPAN) & (r < 3)
    tab[0] = dot(of(1), one_hot(used & (source == r * SPAN + s)))
    total = None
    for j in range(3):
        place = one_hot(used & (r == j) & (source == (2 - j) * SPAN + SPAN - 1 - s))
        part = dot(of(j), place)
        total = part if total is None else total + part
    tab[1] = total


def kernel(
    nlat,
    nlon,
    grid_ref,
    basis_ref,
    widths_ref,
    w1_ref,
    w2_ref,
    cot_ref,
    gin_ref,
    out1_ref,
    out2_ref,
    gext,
    cext,
    basis,
    widths,
    taps,
    tab,
    fband,
    aband,
    w1,
    w2,
    zbuf,
    z1own,
    z2,
    slope,
    hid,
    gact,
    gown,
    part1,
    part2,
    crecv,
    xsend,
    xrecv,
    zown,
    zrecv,
    zall,
    local_sem,
    halo_send,
    halo_recv,
    core_send,
    core_recv,
    x_send,
    x_recv,
    z_send,
    z_recv,
    zg_send,
    zg_recv,
    xg_send,
    xg_recv,
    f_send,
    f_recv,
    z_known,
):
    nx, nz = nlat // 4, nlon // 2
    npl = nx * 4
    xr = HALF // npl
    zr = 2 * xr // nz
    zh = nz // 2
    lat, lon = lax.axis_index("lat"), lax.axis_index("lon")
    core = lat % 2
    z = lon % nz
    me = (lat // 2) * 2 + lon // nz

    def at(la, lo):
        return {"lat": la, "lon": lo}

    plane, line = plane_steps(nx, 4), ring_steps(nz)

    def plane_place(step):
        return ((me // 4 + step[0]) % nx) * 4 + (me + step[1]) % 4

    def in_plane(q):
        return at((q // 2) * 2 + core, (q % 2) * nz + z)

    def in_z(q):
        return at(lat, (lon // nz) * nz + q)

    reach = 1
    z_rounds = []
    while 2 * reach < nz:
        z_rounds.append(reach)
        reach *= 2

    north = (lat == 0).astype(jnp.int32)
    south = (lat == nlat - 1).astype(jnp.int32)
    turn = nlon // 2
    up = (lat - 1 + north, (lon + turn * north) % nlon)
    down = (lat + 1 - south, (lon + turn * south) % nlon)
    sibling = at(lat + 1 - 2 * core, lon)

    def beside(place, step):
        return at(place[0], (place[1] + nlon + step) % nlon)

    up_row = (XR - 2) * (1 - north)
    down_row = (XR - 2) * south
    first, last = slice(0, 2), slice(ROWS - 2, ROWS)
    left, right, every = slice(0, HALO), slice(COLS - HALO, COLS), slice(0, COLS)
    side = (lat, lon)
    neighbours = [
        (beside(up, -1), first, left, up_row, 2, COLS + HALO, HALO),
        (beside(up, 1), first, right, up_row, 2, 0, HALO),
        (beside(down, -1), last, left, down_row, 2, COLS + HALO, HALO),
        (beside(down, 1), last, right, down_row, 2, 0, HALO),
        (at(*up), first, every, up_row, 2, HALO, COLS),
        (at(*down), last, every, down_row, 2, HALO, COLS),
        (beside(side, -1), slice(0, ROWS), left, 2, ROWS, COLS + HALO, HALO),
        (beside(side, 1), slice(0, ROWS), right, 2, ROWS, 0, HALO),
    ]

    own = (
        pltpu.make_async_copy(
            grid_ref, gext.at[pl.ds(2, ROWS), pl.ds(HALO, COLS)], local_sem.at[0]
        ),
        pltpu.make_async_copy(cot_ref, cext.at[pl.ds(2, ROWS), pl.ds(HALO, COLS)], local_sem.at[1]),
        pltpu.make_async_copy(w1_ref, w1, local_sem.at[2]),
        pltpu.make_async_copy(w2_ref, w2, local_sem.at[3]),
        pltpu.make_async_copy(basis_ref, basis, local_sem.at[4]),
        pltpu.make_async_copy(widths_ref, widths, local_sem.at[5]),
    )
    barrier = pltpu.get_barrier_semaphore()

    def signal(device, sem):
        pl.semaphore_signal(sem, inc=1, device_id=device, device_id_type=MESH)

    near = [device for device, *_ in neighbours]
    near += [sibling] + [in_plane(plane_place(step)) for step in plane]
    near += [in_z((z + d) % nz) for d in (line if nz < 4 else (1, nz - 1))]
    for device in near:
        signal(device, barrier)
    for copy in own:
        copy.start()
    pl.semaphore_wait(barrier, len(near))

    def z_signal(n):
        for d in (z_rounds[n], nz - z_rounds[n]):
            signal(in_z((z + d) % nz), z_known.at[n])

    def z_await(n):
        if n < len(z_rounds):
            pl.semaphore_wait(z_known.at[n], 2)
            if n + 1 < len(z_rounds):
                z_signal(n + 1)

    if z_rounds:
        z_signal(0)

    for which, (src, ext) in enumerate(((grid_ref, gext), (cot_ref, cext))):
        for device, rows, cols, row, count, col, width in neighbours:
            pltpu.make_async_remote_copy(
                src_ref=src.at[rows, cols],
                dst_ref=ext.at[pl.ds(row, count), pl.ds(col, width)],
                send_sem=halo_send.at[which],
                recv_sem=halo_recv.at[which],
                device_id=device,
                device_id_type=MESH,
            ).start()

    def await_bytes(ref, sem):
        pltpu.make_async_copy(ref, ref, sem).wait()

    own[4].wait()
    own[5].wait()
    spread_taps(basis, widths, taps, tab, lat, nlat * ROWS)

    def build(which, band):
        def one(v):
            for k in range(KB):
                for h in range(2):
                    row = tab[which, pl.ds(k * SLOT + v, 1), h * 128 : (h + 1) * 128]
                    rolled = pltpu.roll(
                        jnp.broadcast_to(row, (MC, 128)), 0, 1, stride=1, stride_axis=0
                    )
                    band[v, k * MC : (k + 1) * MC, h * 128 : (h + 1) * 128] = rolled.astype(
                        jnp.bfloat16
                    )

        loop(MR, one)

    build(0, fband)
    build(1, aband)
    for buf in (hid, gact):
        buf[:, MC:XC, :] = jnp.zeros((MR, XC - MC, CH), jnp.bfloat16)

    def slot(v):
        if v < 2:
            return v + north * (1 - 2 * v)
        if v >= XR - 2:
            return v + south * (2 * (XR - 2) + 1 - 2 * v)
        return v

    def conv_wide(ext, band, keep_own):
        for v in range(MR):
            rows = jnp.concatenate([ext[slot(v + r)] for r in range(3)], axis=0)
            full = dot(band[v, :, :TAP], rows)
            mixed = full.astype(jnp.bfloat16)
            for k in range(KB):
                zbuf[v * MC : (v + 1) * MC, k * CH : (k + 1) * CH] = mixed[
                    k * MC : (k + 1) * MC, :
                ]
            if keep_own and 1 <= v <= ROWS:
                for k in range(KB):
                    z1own[k, (v - 1) * COLS : v * COLS, :] = full[
                        k * MC + REACH : k * MC + REACH + COLS, :
                    ].astype(jnp.bfloat16)

    def conv_own(src, band, store):
        for i in range(ROWS):
            taps = jnp.concatenate(
                [band[i + 1, k * MC : k * MC + COLS, :TAP] for k in range(KB)], axis=0
            )
            rows = src[i : i + 3].reshape(TAP, CH)
            mixed = dot(taps, rows).astype(jnp.bfloat16)
            for k in range(KB):
                store(i, k, mixed[k * COLS : (k + 1) * COLS, :])

    own[0].wait()
    await_bytes(gext.at[pl.ds(0, ROWS)], halo_recv.at[0])
    z_await(0)
    conv_wide(gext, fband, True)
    own[2].wait()
    act = dot(zbuf[...], w1[...].reshape(KB * CH, CH))
    tanh_val = jnp.tanh(GELU_C * (act + CUBIC * act * act * act))
    slope[...] = 0.5 * (1.0 + tanh_val) + 0.5 * act * (1.0 - tanh_val * tanh_val) * GELU_C * (
        1.0 + 3.0 * CUBIC * act * act
    )
    hidden = (0.5 * act * (1.0 + tanh_val)).astype(jnp.bfloat16)
    for v in range(MR):
        hid[v, :MC, :] = hidden[v * MC : (v + 1) * MC, :]

    def weight_grad(cells, grad, part, g):
        for step in range(KB):
            k = (2 * (1 - core) + step) % KB
            part[k] = t_dot(cells[k], grad)
            if step < 2:
                pltpu.make_async_remote_copy(
                    src_ref=part.at[k],
                    dst_ref=crecv.at[g, step],
                    send_sem=core_send.at[g],
                    recv_sem=core_recv.at[g],
                    device_id=sibling,
                    device_id_type=MESH,
                ).start()

    def store_z2(i, k, value):
        z2[k, i * COLS : (i + 1) * COLS, :] = value

    conv_own(hid, fband, store_z2)
    own[1].wait()
    weight_grad(z2, cext[2 : 2 + ROWS, HALO : HALO + COLS, :].reshape(ROWS * COLS, CH), part2, 1)

    def mix_back(cells, weight):
        total = dot_t(cells[:, :CH], weight[0])
        for k in range(1, KB):
            total = total + dot_t(cells[:, k * CH : (k + 1) * CH], weight[k])
        return total

    await_bytes(cext.at[pl.ds(0, ROWS)], halo_recv.at[1])
    z_await(1)
    conv_wide(cext, aband, False)
    own[3].wait()
    grad_act = mix_back(zbuf, w2) * slope[...]
    for v in range(MR):
        gact[v, :MC, :] = grad_act[v * MC : (v + 1) * MC, :].astype(jnp.bfloat16)
        if 1 <= v <= ROWS:
            gown[(v - 1) * COLS : v * COLS, :] = grad_act[
                v * MC + REACH : v * MC + REACH + COLS, :
            ].astype(jnp.bfloat16)
    weight_grad(z1own, gown[...], part1, 0)

    parts = (part1, part2)
    outs = (out1_ref, out2_ref)
    own_half = 2 * core

    def plane_chunk(g, q):
        k, row = q * xr // CH, (q * xr) % CH
        row = pl.multiple_of(row, xr)
        return parts[g][own_half + k, pl.ds(row, xr), :] + crecv[g, k, pl.ds(row, xr), :]

    def plane_scatter(g):
        await_bytes(crecv.at[g], core_recv.at[g])

        for i, step in enumerate(plane):
            q = plane_place(step)
            xsend[g, i] = plane_chunk(g, q).astype(jnp.bfloat16)
            pltpu.make_async_remote_copy(
                src_ref=xsend.at[g, i],
                dst_ref=xrecv.at[g, i],
                send_sem=x_send.at[g],
                recv_sem=x_recv.at[g],
                device_id=in_plane(q),
                device_id_type=MESH,
            ).start()

    def z_scatter(g):
        total = plane_chunk(g, me)
        await_bytes(xrecv.at[g], x_recv.at[g])
        for i in range(npl - 1):
            total = total + xrecv[g, i].astype(jnp.float32)
        for q in range(nz):
            zown[g, q] = total[
                (q % zh) * zr : (q % zh + 1) * zr, (q // zh) * 128 : (q // zh + 1) * 128
            ]

        for i, d in enumerate(line):
            q = (z + d) % nz
            pltpu.make_async_remote_copy(
                src_ref=zown.at[g, q],
                dst_ref=zrecv.at[g, i],
                send_sem=z_send.at[g],
                recv_sem=z_recv.at[g],
                device_id=in_z(q),
                device_id_type=MESH,
            ).start()

    def z_gather(g):
        total = zown[g, z]
        await_bytes(zrecv.at[g], z_recv.at[g])
        for i in range(nz - 1):
            total = total + zrecv[g, i]
        zall[g, z] = total

        for d in line:
            pltpu.make_async_remote_copy(
                src_ref=zall.at[g, z],
                dst_ref=zall.at[g, z],
                send_sem=zg_send.at[g],
                recv_sem=zg_recv.at[g],
                device_id=in_z((z + d) % nz),
                device_id_type=MESH,
            ).start()

    def plane_gather(g):
        await_bytes(zall.at[g, pl.ds(0, nz - 1)], zg_recv.at[g])
        left = jnp.concatenate([zall[g, q] for q in range(zh)], axis=0)
        right = jnp.concatenate([zall[g, zh + q] for q in range(zh)], axis=0)
        rows = pl.ds(pl.multiple_of(core * HALF + me * xr, xr), xr)
        out = outs[g]
        out[rows, :] = jnp.concatenate([left, right], axis=1).astype(jnp.bfloat16)

        for step in plane:
            pltpu.make_async_remote_copy(
                src_ref=out.at[rows],
                dst_ref=out.at[rows],
                send_sem=xg_send.at[g],
                recv_sem=xg_recv.at[g],
                device_id=in_plane(plane_place(step)),
                device_id_type=MESH,
            ).start()

    def core_gather(g):
        out = outs[g]
        await_bytes(out.at[pl.ds(0, (npl - 1) * xr)], xg_recv.at[g])
        rows = pl.ds(pl.multiple_of(core * HALF, HALF), HALF)
        pltpu.make_async_remote_copy(
            src_ref=out.at[rows],
            dst_ref=out.at[rows],
            send_sem=f_send.at[g],
            recv_sem=f_recv.at[g],
            device_id=sibling,
            device_id_type=MESH,
        ).start()

    plane_scatter(1)
    plane_scatter(0)

    def store_back(i, k, value):
        zbuf[i * COLS : (i + 1) * COLS, k * CH : (k + 1) * CH] = value

    conv_own(gact, aband, store_back)
    gin_ref[...] = mix_back(zbuf.at[pl.ds(0, ROWS * COLS)], w1)

    z_await(2)
    z_scatter(1)
    z_scatter(0)
    z_gather(1)
    z_gather(0)
    plane_gather(1)
    plane_gather(0)
    core_gather(1)
    core_gather(0)
    for which, ext in enumerate((gext, cext)):
        await_bytes(ext.at[pl.ds(0, ROWS)], halo_send.at[which])
    for g in range(2):
        await_bytes(crecv.at[g], core_send.at[g])
        await_bytes(xrecv.at[g], x_send.at[g])
        await_bytes(zrecv.at[g], z_send.at[g])
        await_bytes(zall.at[g, pl.ds(0, nz - 1)], zg_send.at[g])
        await_bytes(outs[g].at[pl.ds(0, (npl - 1) * xr)], xg_send.at[g])
    for g in range(2):
        await_bytes(outs[g].at[pl.ds(0, HALF)], f_recv.at[g])
        await_bytes(outs[g].at[pl.ds(0, HALF)], f_send.at[g])


def widen(g_ref, a_ref, b_ref, g_out, a_out, b_out, a_buf, b_buf, g_sem, ab_sem):
    copies = [pltpu.make_async_copy(g_ref, g_out, g_sem)]
    copies[0].start()
    for n, (ref, buf, out) in enumerate(((a_ref, a_buf, a_out), (b_ref, b_buf, b_out))):
        for k in range(KB):
            buf[k] = ref[k * CH : (k + 1) * CH, :].astype(jnp.float32)
            copies.append(pltpu.make_async_copy(buf.at[k], out.at[k], ab_sem.at[n, k]))
            copies[-1].start()
    for copy in copies:
        copy.wait()


def local(grid_in, basis, widths, weight_one, weight_two, cotangent):
    nlat, nlon = lax.axis_size("lat"), lax.axis_size("lon")
    npl, nz = nlat, nlon // 2
    xr = HALF // npl
    zr = 2 * xr // nz
    bf16, f32 = jnp.bfloat16, jnp.float32
    vmem, dma = pltpu.VMEM, pltpu.SemaphoreType.DMA
    hbm = pl.BlockSpec(memory_space=pltpu.HBM)
    on_chip = pl.BlockSpec(memory_space=pltpu.VMEM)
    nlat_all = basis.shape[0]
    basis = basis.transpose(1, 2, 3, 0).reshape(3 * SPAN, KB, nlat_all)
    grid_in, weight_one, weight_two, cotangent = (
        pltpu.with_memory_space_constraint(x, pltpu.HBM)
        for x in (grid_in, weight_one, weight_two, cotangent)
    )
    basis, widths = (
        pltpu.with_memory_space_constraint(x, pltpu.HBM)
        for x in (basis, widths.reshape(1, nlat_all))
    )
    grad_in, one, two = pl.pallas_call(
        functools.partial(kernel, nlat, nlon),
        out_shape=(
            jax.ShapeDtypeStruct((ROWS * COLS, CH), f32),
            jax.ShapeDtypeStruct((KB * CH, CH), bf16),
            jax.ShapeDtypeStruct((KB * CH, CH), bf16),
        ),
        in_specs=[hbm] * 6,
        out_specs=(on_chip, on_chip, on_chip),
        scratch_shapes=[
            vmem((XR, XC, CH), bf16),
            vmem((XR, XC, CH), bf16),
            vmem((3 * SPAN, KB, nlat_all), bf16),
            vmem((1, nlat_all), jnp.int32),
            vmem((2, KB * TAPS, nlat_all), f32),
            vmem((2, KB * SLOT, 4 * XC), f32),
            vmem((MR, KB * MC, 256), bf16),
            vmem((MR, KB * MC, 256), bf16),
            vmem((KB, CH, CH), bf16),
            vmem((KB, CH, CH), bf16),
            vmem((MR * MC, KB * CH), bf16),
            vmem((KB, ROWS * COLS, CH), bf16),
            vmem((KB, ROWS * COLS, CH), bf16),
            vmem((MR * MC, CH), f32),
            vmem((MR, XC, CH), bf16),
            vmem((MR, XC, CH), bf16),
            vmem((ROWS * COLS, CH), bf16),
            vmem((KB, CH, CH), f32),
            vmem((KB, CH, CH), f32),
            vmem((2, 2, CH, CH), f32),
            vmem((2, npl - 1, xr, CH), bf16),
            vmem((2, npl - 1, xr, CH), bf16),
            vmem((2, nz, zr, 128), f32),
            vmem((2, nz - 1, zr, 128), f32),
            vmem((2, nz, zr, 128), f32),
            dma((6,)),
        ]
        + [dma((2,))] * 14
        + [pltpu.SemaphoreType.REGULAR((3,))],
        compiler_params=pltpu.CompilerParams(
            collective_id=0, has_side_effects=True, vmem_limit_bytes=48 * 1024 * 1024
        ),
    )(grid_in, basis, widths, weight_one, weight_two, cotangent)
    wide = jax.ShapeDtypeStruct(weight_one.shape, f32)
    grad_in, one, two = pl.pallas_call(
        widen,
        out_shape=(jax.ShapeDtypeStruct((ROWS * COLS, CH), f32), wide, wide),
        in_specs=[on_chip] * 3,
        out_specs=(hbm, hbm, hbm),
        scratch_shapes=[vmem(wide.shape, f32), vmem(wide.shape, f32), dma, dma((2, KB))],
        compiler_params=pltpu.CompilerParams(vmem_limit_bytes=16 * 1024 * 1024),
    )(grad_in, one, two)
    return grad_in.reshape(grid_in.shape), one, two


def solution(mesh):
    placed = (P("lat", "lon", None), P(), P(), P(), P(), P("lat", "lon", None))
    return jax.shard_map(
        local,
        mesh=mesh,
        in_specs=placed,
        out_specs=(P("lat", "lon", None), P(), P()),
        check_vma=False,
    )
```

```python
import functools

import jax
import jax.numpy as jnp
from jax import lax
from jax.experimental import pallas as pl
from jax.experimental.pallas import tpu as pltpu
from jax.sharding import PartitionSpec as P

GELU_C = 0.7978845608028654
CUBIC = 0.044715
MESH = pl.DeviceIdType.MESH

ROWS, COLS, CH, KB, REACH = 8, 32, 256, 4, 8
HALO = 2 * REACH
XR, XC = ROWS + 4, COLS + 2 * HALO
MR, MC = ROWS + 2, COLS + 2 * REACH
TAP = 3 * XC
SPAN = 2 * REACH + 1
TAPS = 64
SLOT = 16
HALF = KB * CH // 2


def dot(a, b):
    return jnp.dot(a, b, preferred_element_type=jnp.float32)


def dot_t(a, b):
    return lax.dot_general(a, b, (((1,), (1,)), ((), ())), preferred_element_type=jnp.float32)


def t_dot(a, b):
    return lax.dot_general(a, b, (((0,), (0,)), ((), ())), preferred_element_type=jnp.float32)


def loop(count, body):
    lax.fori_loop(0, count, lambda i, c: (body(i), c)[1], 0, unroll=True)


def tree_sum(terms):
    while len(terms) > 1:
        pairs = [a + b for a, b in zip(terms[::2], terms[1::2])]
        terms = pairs + terms[len(terms) // 2 * 2 :]
    return terms[0]


def ring_offsets(count):
    return [0] + [d * s for d in range(1, count // 2) for s in (1, -1)] + [count // 2]


def ring_groups(count, far):
    cuts = [0, 5 * count // 16, far * count // 16, count]
    return [(a, b - a) for a, b in zip(cuts, cuts[1:])]


def plane_steps(nx, ny):
    steps = [(dx, dy) for dx in range(nx) for dy in range(ny) if dx or dy]
    return sorted(steps, key=lambda s: -min(s[0], nx - s[0]) - min(s[1], ny - s[1]))


def iota(rows, cols, axis):
    return lax.broadcasted_iota(jnp.int32, (rows, cols), axis)


def one_hot(where):
    return where.astype(jnp.float32).astype(jnp.bfloat16)


def spread_taps(basis_ref, widths_ref, taps, tab, lat, nlat_all):
    zeros = jnp.zeros((KB * TAPS, nlat_all), jnp.float32)
    taps[0], taps[1] = zeros, zeros
    widths = widths_ref[...]
    for r in range(3):
        for s in range(SPAN):
            block = basis_ref[r * SPAN + s].astype(jnp.float32)
            block = jnp.where(widths >= abs(s - REACH), block, 0.0)
            taps[0, pl.ds(r * SPAN + s, KB, stride=TAPS), :] = block
            taps[1, pl.ds((2 - r) * SPAN + s, KB, stride=TAPS), :] = block
    picks = []
    for j in range(3):
        row = lat * ROWS - 2 + j + iota(SLOT, nlat_all, 0)
        past = (row < 0) | (row >= nlat_all)
        true_row = jnp.where(row < 0, -1 - row, jnp.where(past, 2 * nlat_all - 1 - row, row))
        hit = true_row == iota(SLOT, nlat_all, 1)
        picks.append((one_hot(hit & jnp.logical_not(past)), one_hot(hit & past)))
    plain = jnp.concatenate([p for p, _ in picks], axis=0)
    mirror = jnp.concatenate([m for _, m in picks], axis=0)
    found = []
    for k in range(KB):
        rows = slice(k * TAPS, (k + 1) * TAPS)
        found.append(
            dot_t(plain, taps[0, rows, :].astype(jnp.bfloat16))
            + dot_t(mirror, taps[1, rows, :].astype(jnp.bfloat16))
        )

    def of(j):
        parts = [f[j * SLOT : (j + 1) * SLOT, :] for f in found]
        return jnp.concatenate(parts, axis=0).astype(jnp.bfloat16)

    source, lane = iota(TAPS, 4 * XC, 0), iota(TAPS, 4 * XC, 1)
    r, s = lane // XC, lane % XC
    used = (s < SPAN) & (r < 3)
    tab[0] = dot(of(1), one_hot(used & (source == r * SPAN + s)))
    total = None
    for j in range(3):
        place = one_hot(used & (r == j) & (source == (2 - j) * SPAN + SPAN - 1 - s))
        part = dot(of(j), place)
        total = part if total is None else total + part
    tab[1] = total


def kernel(
    nlat,
    nlon,
    grid_ref,
    basis_ref,
    widths_ref,
    w1_ref,
    w2_ref,
    cot_ref,
    gin_ref,
    sums_ref,
    gext,
    cext,
    basis,
    widths,
    taps,
    tab,
    fband,
    aband,
    w1,
    w2,
    zbuf,
    z1own,
    z2,
    slope,
    hid,
    gact,
    gown,
    part1,
    part2,
    crecv,
    xsend,
    xrecv,
    xown,
    zsend,
    zrecv,
    out,
    local_sem,
    halo_send,
    halo_recv,
    core_send,
    core_recv,
    x_send,
    x_recv,
    z_send,
    z_recv,
    zg_send,
    zg_recv,
    xg_send,
    xg_recv,
    f_send,
    f_recv,
    z_known,
):
    nx, nz = nlat // 4, nlon // 2
    npl = nx * 4
    xr = 2 * HALF // npl
    zh = nz // 2
    zr = xr // zh
    lat, lon = lax.axis_index("lat"), lax.axis_index("lon")
    core = lat % 2
    z = lon % nz
    me = (lat // 2) * 2 + lon // nz

    def at(la, lo):
        return {"lat": la, "lon": lo}

    plane = plane_steps(nx, 4)
    offsets, groups, last_groups = ring_offsets(nz), ring_groups(nz, 11), ring_groups(nz, 13)

    def plane_place(step):
        return ((me // 4 + step[0]) % nx) * 4 + (me + step[1]) % 4

    def in_plane(q, side=core):
        return at((q // 2) * 2 + side, (q % 2) * nz + z)

    def in_z(q):
        return at(lat, (lon // nz) * nz + q)

    reach = 1
    z_rounds = []
    while 2 * reach < nz:
        z_rounds.append(reach)
        reach *= 2

    north = (lat == 0).astype(jnp.int32)
    south = (lat == nlat - 1).astype(jnp.int32)
    turn = nlon // 2
    up = (lat - 1 + north, (lon + turn * north) % nlon)
    down = (lat + 1 - south, (lon + turn * south) % nlon)
    sibling = at(lat + 1 - 2 * core, lon)

    def beside(place, step):
        return at(place[0], (place[1] + nlon + step) % nlon)

    up_row = (XR - 2) * (1 - north)
    down_row = (XR - 2) * south
    first, last = slice(0, 2), slice(ROWS - 2, ROWS)
    left, right, every = slice(0, HALO), slice(COLS - HALO, COLS), slice(0, COLS)
    side = (lat, lon)
    neighbours = [
        (beside(up, -1), first, left, up_row, 2, COLS + HALO, HALO),
        (beside(up, 1), first, right, up_row, 2, 0, HALO),
        (beside(down, -1), last, left, down_row, 2, COLS + HALO, HALO),
        (beside(down, 1), last, right, down_row, 2, 0, HALO),
        (at(*up), first, every, up_row, 2, HALO, COLS),
        (at(*down), last, every, down_row, 2, HALO, COLS),
        (beside(side, -1), slice(0, ROWS), left, 2, ROWS, COLS + HALO, HALO),
        (beside(side, 1), slice(0, ROWS), right, 2, ROWS, 0, HALO),
    ]

    own = (
        pltpu.make_async_copy(
            grid_ref, gext.at[pl.ds(2, ROWS), pl.ds(HALO, COLS)], local_sem.at[0]
        ),
        pltpu.make_async_copy(cot_ref, cext.at[pl.ds(2, ROWS), pl.ds(HALO, COLS)], local_sem.at[1]),
        pltpu.make_async_copy(w1_ref, w1, local_sem.at[2]),
        pltpu.make_async_copy(w2_ref, w2, local_sem.at[3]),
        pltpu.make_async_copy(basis_ref, basis, local_sem.at[4]),
        pltpu.make_async_copy(widths_ref, widths, local_sem.at[5]),
    )
    barrier = pltpu.get_barrier_semaphore()

    def signal(device, sem):
        pl.semaphore_signal(sem, inc=1, device_id=device, device_id_type=MESH)

    near = [device for device, *_ in neighbours]
    near += [sibling] + [in_plane(plane_place(step)) for step in plane]
    near += [in_z((z + d) % nz) for d in (1, nz - 1)]
    for device in near:
        signal(device, barrier)
    for copy in own:
        copy.start()
    pl.semaphore_wait(barrier, len(near))

    def z_signal(n):
        for d in (z_rounds[n], nz - z_rounds[n]):
            signal(in_z((z + d) % nz), z_known.at[n])

    def z_await(n):
        if n < len(z_rounds):
            pl.semaphore_wait(z_known.at[n], 2)
            if n + 1 < len(z_rounds):
                z_signal(n + 1)

    if z_rounds:
        z_signal(0)

    for which, (src, ext) in enumerate(((grid_ref, gext), (cot_ref, cext))):
        for device, rows, cols, row, count, col, width in neighbours:
            pltpu.make_async_remote_copy(
                src_ref=src.at[rows, cols],
                dst_ref=ext.at[pl.ds(row, count), pl.ds(col, width)],
                send_sem=halo_send.at[which],
                recv_sem=halo_recv.at[which],
                device_id=device,
                device_id_type=MESH,
            ).start()

    def await_bytes(ref, sem):
        pltpu.make_async_copy(ref, ref, sem).wait()

    own[4].wait()
    own[5].wait()
    spread_taps(basis, widths, taps, tab, lat, nlat * ROWS)

    def build(which, band):
        def one(v):
            for k in range(KB):
                for h in range(2):
                    row = tab[which, pl.ds(k * SLOT + v, 1), h * 128 : (h + 1) * 128]
                    rolled = pltpu.roll(
                        jnp.broadcast_to(row, (MC, 128)), 0, 1, stride=1, stride_axis=0
                    )
                    band[v, k * MC : (k + 1) * MC, h * 128 : (h + 1) * 128] = rolled.astype(
                        jnp.bfloat16
                    )

        loop(MR, one)

    build(0, fband)
    build(1, aband)
    for buf in (hid, gact):
        buf[:, MC:XC, :] = jnp.zeros((MR, XC - MC, CH), jnp.bfloat16)

    def slot(v):
        if v < 2:
            return v + north * (1 - 2 * v)
        if v >= XR - 2:
            return v + south * (2 * (XR - 2) + 1 - 2 * v)
        return v

    def conv_wide(ext, band, keep_own):
        for v in range(MR):
            rows = jnp.concatenate([ext[slot(v + r)] for r in range(3)], axis=0)
            full = dot(band[v, :, :TAP], rows)
            mixed = full.astype(jnp.bfloat16)
            for k in range(KB):
                zbuf[v * MC : (v + 1) * MC, k * CH : (k + 1) * CH] = mixed[
                    k * MC : (k + 1) * MC, :
                ]
            if keep_own and 1 <= v <= ROWS:
                for k in range(KB):
                    z1own[k, (v - 1) * COLS : v * COLS, :] = full[
                        k * MC + REACH : k * MC + REACH + COLS, :
                    ].astype(jnp.bfloat16)

    def conv_own(src, band, store):
        for i in range(ROWS):
            taps = jnp.concatenate(
                [band[i + 1, k * MC : k * MC + COLS, :TAP] for k in range(KB)], axis=0
            )
            rows = src[i : i + 3].reshape(TAP, CH)
            mixed = dot(taps, rows).astype(jnp.bfloat16)
            for k in range(KB):
                store(i, k, mixed[k * COLS : (k + 1) * COLS, :])

    own[0].wait()
    await_bytes(gext.at[pl.ds(0, ROWS)], halo_recv.at[0])
    z_await(0)
    conv_wide(gext, fband, True)
    own[2].wait()
    act = dot(zbuf[...], w1[...].reshape(KB * CH, CH))
    tanh_val = jnp.tanh(GELU_C * (act + CUBIC * act * act * act))
    slope[...] = 0.5 * (1.0 + tanh_val) + 0.5 * act * (1.0 - tanh_val * tanh_val) * GELU_C * (
        1.0 + 3.0 * CUBIC * act * act
    )
    hidden = (0.5 * act * (1.0 + tanh_val)).astype(jnp.bfloat16)
    for v in range(MR):
        hid[v, :MC, :] = hidden[v * MC : (v + 1) * MC, :]

    def weight_grad(cells, grad, part, g):
        for step in range(KB):
            k = (2 * (1 - core) + step) % KB
            part[k] = t_dot(cells[k], grad)
            if step < 2:
                pltpu.make_async_remote_copy(
                    src_ref=part.at[k],
                    dst_ref=crecv.at[g, step],
                    send_sem=core_send.at[g],
                    recv_sem=core_recv.at[g],
                    device_id=sibling,
                    device_id_type=MESH,
                ).start()

    def store_z2(i, k, value):
        z2[k, i * COLS : (i + 1) * COLS, :] = value

    conv_own(hid, fband, store_z2)
    own[1].wait()
    weight_grad(z2, cext[2 : 2 + ROWS, HALO : HALO + COLS, :].reshape(ROWS * COLS, CH), part2, 0)

    def mix_back(cells, weight):
        total = dot_t(cells[:, :CH], weight[0])
        for k in range(1, KB):
            total = total + dot_t(cells[:, k * CH : (k + 1) * CH], weight[k])
        return total

    await_bytes(cext.at[pl.ds(0, ROWS)], halo_recv.at[1])
    z_await(1)
    conv_wide(cext, aband, False)
    own[3].wait()
    grad_act = mix_back(zbuf, w2) * slope[...]
    for v in range(MR):
        gact[v, :MC, :] = grad_act[v * MC : (v + 1) * MC, :].astype(jnp.bfloat16)
        if 1 <= v <= ROWS:
            gown[(v - 1) * COLS : v * COLS, :] = grad_act[
                v * MC + REACH : v * MC + REACH + COLS, :
            ].astype(jnp.bfloat16)
    weight_grad(z1own, gown[...], part1, 1)

    parts = (part2, part1)
    own_half = 2 * core

    def place_of(q):
        offset = (q - z + nz + zh) % nz - zh
        ahead = (offset > 0).astype(jnp.int32)
        behind = (offset < 0).astype(jnp.int32)
        far = (offset == -zh).astype(jnp.int32)
        return 2 * offset * (ahead - behind) - ahead - far

    places = [place_of(q) for q in range(nz)]

    def plane_chunk(p, store):
        row = (p // 2) * xr
        k, row = row // CH, pl.multiple_of(row % CH, xr)
        lanes = pl.ds(pl.multiple_of((p % 2) * 128, 128), 128)
        for g in range(2):
            rows = pl.ds(row, xr)
            total = parts[g][own_half + k, rows, lanes] + crecv[g, k, rows, lanes]
            for i in range(zh):
                store(places[g * zh + i], total[i * zr : (i + 1) * zr, :])

    def plane_send(slot, group):
        first, count = groups[group]
        some = pl.ds(first, count)
        pltpu.make_async_remote_copy(
            src_ref=xsend.at[slot, some],
            dst_ref=xrecv.at[slot, some],
            send_sem=x_send.at[group],
            recv_sem=x_recv.at[group],
            device_id=in_plane(plane_place(plane[slot])),
            device_id_type=MESH,
        ).start()

    def plane_scatter():
        for g in range(2):
            await_bytes(crecv.at[g], core_recv.at[g])
        for slot, step in enumerate(plane):

            def store(place, value, slot=slot):
                xsend[slot, place] = value.astype(jnp.bfloat16)

            plane_chunk(plane_place(step), store)
            plane_send(slot, len(groups) - 1)
        for group in (1, 0):
            for slot in range(len(plane)):
                plane_send(slot, group)

        def keep(place, value):
            xown[place] = value

        plane_chunk(me, keep)

    def z_scatter(group):
        first, count = groups[group]
        await_bytes(xrecv.at[:, pl.ds(first, count)], x_recv.at[group])
        terms = [xown[pl.ds(first, count)]]
        terms += [xrecv[s, pl.ds(first, count)].astype(jnp.float32) for s in range(len(plane))]
        zsend[pl.ds(first, count)] = tree_sum(terms)
        for place in reversed(range(first, first + count)):
            if place > 0:
                pltpu.make_async_remote_copy(
                    src_ref=zsend.at[place],
                    dst_ref=zrecv.at[place - 1],
                    send_sem=z_send.at[0],
                    recv_sem=z_recv.at[0],
                    device_id=in_z((z + nz + offsets[place]) % nz),
                    device_id_type=MESH,
                ).start()

    def z_gather():
        await_bytes(zrecv, z_recv.at[0])
        total = tree_sum([zsend[0]] + [zrecv[place] for place in range(nz - 1)])
        out[core, me, 0] = total.astype(jnp.bfloat16)
        for place in reversed(range(1, nz)):
            there = offsets.index(-offsets[place]) if 2 * offsets[place] < nz else place
            group = sum(there >= first for first, _ in last_groups) - 1
            pltpu.make_async_remote_copy(
                src_ref=out.at[core, me, 0],
                dst_ref=out.at[core, me, there],
                send_sem=zg_send.at[0],
                recv_sem=zg_recv.at[group],
                device_id=in_z((z + nz + offsets[place]) % nz),
                device_id_type=MESH,
            ).start()

    def gather(src, device, send, recv):
        pltpu.make_async_remote_copy(
            src_ref=src,
            dst_ref=src,
            send_sem=send,
            recv_sem=recv,
            device_id=device,
            device_id_type=MESH,
        ).start()

    def plane_gather(group):
        first, count = last_groups[group]
        own_chunk = 1 if first == 0 else 0
        if count > own_chunk:
            arrived = out.at[core, me, pl.ds(first + own_chunk, count - own_chunk)]
            await_bytes(arrived, zg_recv.at[group])
        some = out.at[core, me, pl.ds(first, count)]
        for step in plane:
            q = plane_place(step)
            gather(some, in_plane(q), xg_send.at[group], xg_recv.at[group])
            if group == 2:
                gather(some, in_plane(q, 1 - core), f_send.at[group], f_recv.at[group])
        if group == 2:
            gather(some, sibling, f_send.at[group], f_recv.at[group])

    def of_group(half, group, chips):
        first, count = last_groups[group]
        return out.at[half, pl.ds(0, chips), pl.ds(first, count)]

    q_of = [(z + nz + offset) % nz for offset in offsets]
    grad_of = [q // zh for q in q_of]
    row_of = [pl.multiple_of((q % zh) * zr, zr) for q in q_of]

    def emit(half, group):
        first, count = last_groups[group]
        for p in range(npl):
            k, base = (p // 2) * xr // CH, (p // 2) * xr % CH
            lanes = slice((p % 2) * 128, (p % 2 + 1) * 128)
            for place in range(first, first + count):
                rows = pl.ds(base + row_of[place], zr)
                sums_ref[grad_of[place], 2 * half + k, rows, lanes] = out[half, p, place].astype(
                    jnp.float32
                )

    def core_gather(group):
        await_bytes(of_group(core, group, npl - 1), xg_recv.at[group])
        if group < 2:
            gather(of_group(core, group, npl), sibling, f_send.at[group], f_recv.at[group])
        emit(core, group)

    def finish(group):
        await_bytes(of_group(core, group, npl), f_recv.at[group])
        emit(1 - core, group)

    plane_scatter()

    def store_back(i, k, value):
        zbuf[i * COLS : (i + 1) * COLS, k * CH : (k + 1) * CH] = value

    conv_own(gact, aband, store_back)
    gin_ref[...] = mix_back(zbuf.at[pl.ds(0, ROWS * COLS)], w1)

    z_await(2)
    for group in reversed(range(len(groups))):
        z_scatter(group)
    z_gather()
    for group in range(3):
        plane_gather(group)
    core_gather(0)
    core_gather(1)
    finish(0)
    finish(1)
    for which, ext in enumerate((gext, cext)):
        await_bytes(ext.at[pl.ds(0, ROWS)], halo_send.at[which])
    for g in range(2):
        await_bytes(crecv.at[g], core_send.at[g])
    await_bytes(zrecv, z_send.at[0])
    await_bytes(out.at[core, me, pl.ds(0, nz - 1)], zg_send.at[0])
    for group, (first, count) in enumerate(groups):
        await_bytes(xrecv.at[:, pl.ds(first, count)], x_send.at[group])
    for group in range(2):
        await_bytes(of_group(core, group, npl - 1), xg_send.at[group])
        await_bytes(of_group(core, group, npl), f_send.at[group])
    core_gather(2)
    finish(2)
    await_bytes(of_group(core, 2, npl - 1), xg_send.at[2])
    await_bytes(of_group(core, 2, npl), f_send.at[2])


def write_out(g_ref, sums_ref, g_out, one_out, two_out, g_sem, sem):
    copies = [pltpu.make_async_copy(g_ref, g_out, g_sem)]
    for n, out in enumerate((two_out, one_out)):
        for k in range(KB):
            copies.append(pltpu.make_async_copy(sums_ref.at[n, k], out.at[k], sem.at[n, k]))
    for copy in copies:
        copy.start()
    for copy in copies:
        copy.wait()


def local(grid_in, basis, widths, weight_one, weight_two, cotangent):
    nlat, nlon = lax.axis_size("lat"), lax.axis_size("lon")
    npl, nz = nlat, nlon // 2
    zr = 4 * HALF // (npl * nz)
    bf16, f32 = jnp.bfloat16, jnp.float32
    vmem, dma = pltpu.VMEM, pltpu.SemaphoreType.DMA
    hbm = pl.BlockSpec(memory_space=pltpu.HBM)
    on_chip = pl.BlockSpec(memory_space=pltpu.VMEM)
    nlat_all = basis.shape[0]
    basis = basis.transpose(1, 2, 3, 0).reshape(3 * SPAN, KB, nlat_all)
    grid_in, weight_one, weight_two, cotangent = (
        pltpu.with_memory_space_constraint(x, pltpu.HBM)
        for x in (grid_in, weight_one, weight_two, cotangent)
    )
    basis, widths = (
        pltpu.with_memory_space_constraint(x, pltpu.HBM)
        for x in (basis, widths.reshape(1, nlat_all))
    )
    grad_in, sums = pl.pallas_call(
        functools.partial(kernel, nlat, nlon),
        out_shape=(
            jax.ShapeDtypeStruct((ROWS * COLS, CH), f32),
            jax.ShapeDtypeStruct((2, KB, CH, CH), f32),
        ),
        in_specs=[hbm] * 6,
        out_specs=(on_chip, on_chip),
        scratch_shapes=[
            vmem((XR, XC, CH), bf16),
            vmem((XR, XC, CH), bf16),
            vmem((3 * SPAN, KB, nlat_all), bf16),
            vmem((1, nlat_all), jnp.int32),
            vmem((2, KB * TAPS, nlat_all), f32),
            vmem((2, KB * SLOT, 4 * XC), f32),
            vmem((MR, KB * MC, 256), bf16),
            vmem((MR, KB * MC, 256), bf16),
            vmem((KB, CH, CH), bf16),
            vmem((KB, CH, CH), bf16),
            vmem((MR * MC, KB * CH), bf16),
            vmem((KB, ROWS * COLS, CH), bf16),
            vmem((KB, ROWS * COLS, CH), bf16),
            vmem((MR * MC, CH), f32),
            vmem((MR, XC, CH), bf16),
            vmem((MR, XC, CH), bf16),
            vmem((ROWS * COLS, CH), bf16),
            vmem((KB, CH, CH), f32),
            vmem((KB, CH, CH), f32),
            vmem((2, 2, CH, CH), f32),
            vmem((npl - 1, nz, zr, 128), bf16),
            vmem((npl - 1, nz, zr, 128), bf16),
            vmem((nz, zr, 128), f32),
            vmem((nz, zr, 128), f32),
            vmem((nz - 1, zr, 128), f32),
            vmem((2, npl, nz, zr, 128), bf16),
            dma((6,)),
        ]
        + [dma((2,))] * 4
        + [dma((3,))] * 10
        + [pltpu.SemaphoreType.REGULAR((3,))],
        compiler_params=pltpu.CompilerParams(
            collective_id=0, has_side_effects=True, vmem_limit_bytes=48 * 1024 * 1024
        ),
    )(grid_in, basis, widths, weight_one, weight_two, cotangent)
    wide = jax.ShapeDtypeStruct(weight_one.shape, f32)
    grad_in, one, two = pl.pallas_call(
        write_out,
        out_shape=(jax.ShapeDtypeStruct((ROWS * COLS, CH), f32), wide, wide),
        in_specs=[on_chip] * 2,
        out_specs=(hbm, hbm, hbm),
        scratch_shapes=[dma, dma((2, KB))],
        compiler_params=pltpu.CompilerParams(vmem_limit_bytes=16 * 1024 * 1024),
    )(grad_in, sums)
    return grad_in.reshape(grid_in.shape), one, two


def solution(mesh):
    placed = (P("lat", "lon", None), P(), P(), P(), P(), P("lat", "lon", None))
    return jax.shard_map(
        local,
        mesh=mesh,
        in_specs=placed,
        out_specs=(P("lat", "lon", None), P(), P()),
        check_vma=False,
    )
```

```python
import functools

import jax
import jax.numpy as jnp
from jax import lax
from jax.experimental import pallas as pl
from jax.experimental.pallas import tpu as pltpu
from jax.sharding import PartitionSpec as P

GELU_C = 0.7978845608028654
CUBIC = 0.044715
MESH = pl.DeviceIdType.MESH

ROWS, COLS, CH, KB, REACH = 8, 32, 256, 4, 8
HALO = 2 * REACH
XR, XC = ROWS + 4, COLS + 2 * HALO
MR, MC = ROWS + 2, COLS + 2 * REACH
TAP = 3 * XC
SPAN = 2 * REACH + 1
TAPS = 64
SLOT = 16
HALF = KB * CH // 2


def dot(a, b):
    return jnp.dot(a, b, preferred_element_type=jnp.float32)


def dot_t(a, b):
    return lax.dot_general(a, b, (((1,), (1,)), ((), ())), preferred_element_type=jnp.float32)


def t_dot(a, b):
    return lax.dot_general(a, b, (((0,), (0,)), ((), ())), preferred_element_type=jnp.float32)


def loop(count, body):
    lax.fori_loop(0, count, lambda i, c: (body(i), c)[1], 0, unroll=True)


def tree_sum(terms):
    while len(terms) > 1:
        pairs = [a + b for a, b in zip(terms[::2], terms[1::2])]
        terms = pairs + terms[len(terms) // 2 * 2 :]
    return terms[0]


def ring_offsets(count):
    return [0] + [d * s for d in range(1, count // 2) for s in (1, -1)] + [count // 2]


def ring_groups(count, near, far):
    cuts = [0, near * count // 16, far * count // 16, count]
    return [(a, b - a) for a, b in zip(cuts, cuts[1:])]


def plane_steps(nx, ny):
    steps = [(dx, dy) for dx in range(nx) for dy in range(ny) if dx or dy]
    return sorted(steps, key=lambda s: -min(s[0], nx - s[0]) - min(s[1], ny - s[1]))


def iota(rows, cols, axis):
    return lax.broadcasted_iota(jnp.int32, (rows, cols), axis)


def one_hot(where):
    return where.astype(jnp.float32).astype(jnp.bfloat16)


def spread_taps(basis_ref, widths_ref, taps, tab, lat, nlat_all):
    zeros = jnp.zeros((KB * TAPS, nlat_all), jnp.float32)
    taps[0], taps[1] = zeros, zeros
    widths = widths_ref[...]
    for r in range(3):
        for s in range(SPAN):
            block = basis_ref[r * SPAN + s].astype(jnp.float32)
            block = jnp.where(widths >= abs(s - REACH), block, 0.0)
            taps[0, pl.ds(r * SPAN + s, KB, stride=TAPS), :] = block
            taps[1, pl.ds((2 - r) * SPAN + s, KB, stride=TAPS), :] = block
    picks = []
    for j in range(3):
        row = lat * ROWS - 2 + j + iota(SLOT, nlat_all, 0)
        past = (row < 0) | (row >= nlat_all)
        true_row = jnp.where(row < 0, -1 - row, jnp.where(past, 2 * nlat_all - 1 - row, row))
        hit = true_row == iota(SLOT, nlat_all, 1)
        picks.append((one_hot(hit & jnp.logical_not(past)), one_hot(hit & past)))
    plain = jnp.concatenate([p for p, _ in picks], axis=0)
    mirror = jnp.concatenate([m for _, m in picks], axis=0)
    found = []
    for k in range(KB):
        rows = slice(k * TAPS, (k + 1) * TAPS)
        found.append(
            dot_t(plain, taps[0, rows, :].astype(jnp.bfloat16))
            + dot_t(mirror, taps[1, rows, :].astype(jnp.bfloat16))
        )

    def of(j):
        parts = [f[j * SLOT : (j + 1) * SLOT, :] for f in found]
        return jnp.concatenate(parts, axis=0).astype(jnp.bfloat16)

    source, lane = iota(TAPS, 4 * XC, 0), iota(TAPS, 4 * XC, 1)
    r, s = lane // XC, lane % XC
    used = (s < SPAN) & (r < 3)
    tab[0] = dot(of(1), one_hot(used & (source == r * SPAN + s)))
    total = None
    for j in range(3):
        place = one_hot(used & (r == j) & (source == (2 - j) * SPAN + SPAN - 1 - s))
        part = dot(of(j), place)
        total = part if total is None else total + part
    tab[1] = total


def kernel(
    nlat,
    nlon,
    grid_ref,
    basis_ref,
    widths_ref,
    w1_ref,
    w2_ref,
    cot_ref,
    gin_ref,
    sums_ref,
    gext,
    cext,
    basis,
    widths,
    taps,
    tab,
    fband,
    aband,
    w1,
    w2,
    zbuf,
    z1own,
    z2,
    slope,
    hid,
    gact,
    gown,
    part1,
    part2,
    csend,
    crecv,
    xsend,
    xrecv,
    xown,
    zsend,
    zrecv,
    out,
    local_sem,
    halo_send,
    halo_recv,
    core_send,
    core_recv,
    x_send,
    x_recv,
    z_send,
    z_recv,
    zg_send,
    zg_recv,
    xg_send,
    xg_recv,
    f_send,
    f_recv,
    z_known,
):
    nx, nz = nlat // 4, nlon // 2
    npl = nx * 4
    xr = 2 * HALF // npl
    zh = nz // 2
    zr = xr // zh
    lat, lon = lax.axis_index("lat"), lax.axis_index("lon")
    core = lat % 2
    z = lon % nz
    me = (lat // 2) * 2 + lon // nz

    def at(la, lo):
        return {"lat": la, "lon": lo}

    plane = plane_steps(nx, 4)
    offsets, groups, last_groups = ring_offsets(nz), ring_groups(nz, 5, 11), ring_groups(nz, 7, 13)

    def plane_place(step):
        return ((me // 4 + step[0]) % nx) * 4 + (me + step[1]) % 4

    def in_plane(q, side=core):
        return at((q // 2) * 2 + side, (q % 2) * nz + z)

    def in_z(q):
        return at(lat, (lon // nz) * nz + q)

    reach = 1
    z_rounds = []
    while 2 * reach < nz:
        z_rounds.append(reach)
        reach *= 2

    north = (lat == 0).astype(jnp.int32)
    south = (lat == nlat - 1).astype(jnp.int32)
    turn = nlon // 2
    up = (lat - 1 + north, (lon + turn * north) % nlon)
    down = (lat + 1 - south, (lon + turn * south) % nlon)
    sibling = at(lat + 1 - 2 * core, lon)

    def beside(place, step):
        return at(place[0], (place[1] + nlon + step) % nlon)

    up_row = (XR - 2) * (1 - north)
    down_row = (XR - 2) * south
    first, last = slice(0, 2), slice(ROWS - 2, ROWS)
    left, right, every = slice(0, HALO), slice(COLS - HALO, COLS), slice(0, COLS)
    side = (lat, lon)
    neighbours = [
        (beside(up, -1), first, left, up_row, 2, COLS + HALO, HALO),
        (beside(up, 1), first, right, up_row, 2, 0, HALO),
        (beside(down, -1), last, left, down_row, 2, COLS + HALO, HALO),
        (beside(down, 1), last, right, down_row, 2, 0, HALO),
        (at(*up), first, every, up_row, 2, HALO, COLS),
        (at(*down), last, every, down_row, 2, HALO, COLS),
        (beside(side, -1), slice(0, ROWS), left, 2, ROWS, COLS + HALO, HALO),
        (beside(side, 1), slice(0, ROWS), right, 2, ROWS, 0, HALO),
    ]

    own = (
        pltpu.make_async_copy(
            grid_ref, gext.at[pl.ds(2, ROWS), pl.ds(HALO, COLS)], local_sem.at[0]
        ),
        pltpu.make_async_copy(cot_ref, cext.at[pl.ds(2, ROWS), pl.ds(HALO, COLS)], local_sem.at[1]),
        pltpu.make_async_copy(w1_ref, w1, local_sem.at[2]),
        pltpu.make_async_copy(w2_ref, w2, local_sem.at[3]),
        pltpu.make_async_copy(basis_ref, basis, local_sem.at[4]),
        pltpu.make_async_copy(widths_ref, widths, local_sem.at[5]),
    )
    barrier = pltpu.get_barrier_semaphore()

    def signal(device, sem):
        pl.semaphore_signal(sem, inc=1, device_id=device, device_id_type=MESH)

    near = [device for device, *_ in neighbours]
    near += [sibling] + [in_plane(plane_place(step)) for step in plane]
    near += [in_z((z + d) % nz) for d in (1, nz - 1)]
    for device in near:
        signal(device, barrier)
    for copy in own:
        copy.start()
    pl.semaphore_wait(barrier, len(near))

    def z_signal(n):
        for d in (z_rounds[n], nz - z_rounds[n]):
            signal(in_z((z + d) % nz), z_known.at[n])

    def z_await(n):
        if n < len(z_rounds):
            pl.semaphore_wait(z_known.at[n], 2)
            if n + 1 < len(z_rounds):
                z_signal(n + 1)

    if z_rounds:
        z_signal(0)

    for which, (src, ext) in enumerate(((grid_ref, gext), (cot_ref, cext))):
        for n, (device, rows, cols, row, count, col, width) in enumerate(neighbours):
            beside_us = which + 2 * (n >= 6)
            pltpu.make_async_remote_copy(
                src_ref=src.at[rows, cols],
                dst_ref=ext.at[pl.ds(row, count), pl.ds(col, width)],
                send_sem=halo_send.at[beside_us],
                recv_sem=halo_recv.at[beside_us],
                device_id=device,
                device_id_type=MESH,
            ).start()

    def await_bytes(ref, sem):
        pltpu.make_async_copy(ref, ref, sem).wait()

    own[4].wait()
    own[5].wait()
    spread_taps(basis, widths, taps, tab, lat, nlat * ROWS)

    def build(which, band):
        def one(v):
            for k in range(KB):
                for h in range(2):
                    row = tab[which, pl.ds(k * SLOT + v, 1), h * 128 : (h + 1) * 128]
                    rolled = pltpu.roll(
                        jnp.broadcast_to(row, (MC, 128)), 0, 1, stride=1, stride_axis=0
                    )
                    band[v, k * MC : (k + 1) * MC, h * 128 : (h + 1) * 128] = rolled.astype(
                        jnp.bfloat16
                    )

        loop(MR, one)

    build(0, fband)
    build(1, aband)
    for buf in (hid, gact):
        buf[:, MC:XC, :] = jnp.zeros((MR, XC - MC, CH), jnp.bfloat16)

    def slot(v):
        if v < 2:
            return v + north * (1 - 2 * v)
        if v >= XR - 2:
            return v + south * (2 * (XR - 2) + 1 - 2 * v)
        return v

    inner, outer = range(2, MR - 2), (0, 1, MR - 2, MR - 1)

    def conv_wide(ext, band, keep_own, some):
        for v in some:
            rows = jnp.concatenate([ext[slot(v + r)] for r in range(3)], axis=0)
            full = dot(band[v, :, :TAP], rows)
            mixed = full.astype(jnp.bfloat16)
            for k in range(KB):
                zbuf[v * MC : (v + 1) * MC, k * CH : (k + 1) * CH] = mixed[
                    k * MC : (k + 1) * MC, :
                ]
            if keep_own and 1 <= v <= ROWS:
                for k in range(KB):
                    z1own[k, (v - 1) * COLS : v * COLS, :] = full[
                        k * MC + REACH : k * MC + REACH + COLS, :
                    ].astype(jnp.bfloat16)

    def cells(buf, some):
        if some is inner:
            return buf[2 * MC : (MR - 2) * MC, :]
        return jnp.concatenate([buf[: 2 * MC, :], buf[(MR - 2) * MC :, :]], axis=0)

    def conv_own(src, band, store):
        for i in range(ROWS):
            taps = jnp.concatenate(
                [band[i + 1, k * MC : k * MC + COLS, :TAP] for k in range(KB)], axis=0
            )
            rows = src[i : i + 3].reshape(TAP, CH)
            mixed = dot(taps, rows).astype(jnp.bfloat16)
            for k in range(KB):
                store(i, k, mixed[k * COLS : (k + 1) * COLS, :])

    def forward(some):
        conv_wide(gext, fband, True, some)
        act = dot(cells(zbuf, some), w1[...].reshape(KB * CH, CH))
        tanh_val = jnp.tanh(GELU_C * (act + CUBIC * act * act * act))
        slopes = 0.5 * (1.0 + tanh_val) + 0.5 * act * (1.0 - tanh_val * tanh_val) * GELU_C * (
            1.0 + 3.0 * CUBIC * act * act
        )
        hidden = (0.5 * act * (1.0 + tanh_val)).astype(jnp.bfloat16)
        for n, v in enumerate(some):
            slope[v * MC : (v + 1) * MC, :] = slopes[n * MC : (n + 1) * MC, :]
            hid[v, :MC, :] = hidden[n * MC : (n + 1) * MC, :]

    def mix_back(total_cells, weight):
        total = dot_t(total_cells[:, :CH], weight[0])
        for k in range(1, KB):
            total = total + dot_t(total_cells[:, k * CH : (k + 1) * CH], weight[k])
        return total

    def backward(some):
        conv_wide(cext, aband, False, some)
        grad_act = mix_back(cells(zbuf, some), w2) * cells(slope, some)
        for n, v in enumerate(some):
            gact[v, :MC, :] = grad_act[n * MC : (n + 1) * MC, :].astype(jnp.bfloat16)
            if 1 <= v <= ROWS:
                gown[(v - 1) * COLS : v * COLS, :] = grad_act[
                    n * MC + REACH : n * MC + REACH + COLS, :
                ].astype(jnp.bfloat16)

    own[0].wait()
    await_bytes(gext.at[pl.ds(0, ROWS), pl.ds(0, 2 * HALO)], halo_recv.at[2])
    z_await(0)
    own[2].wait()
    forward(inner)
    own[1].wait()
    await_bytes(cext.at[pl.ds(0, ROWS), pl.ds(0, 2 * HALO)], halo_recv.at[3])
    own[3].wait()
    backward(inner)
    await_bytes(gext.at[pl.ds(0, 4)], halo_recv.at[0])
    z_await(1)
    forward(outer)

    def weight_grad(cells, grad, part, g):
        for step in range(KB):
            k = (2 * (1 - core) + step) % KB
            value = t_dot(cells[k], grad)
            if step >= 2:
                part[k] = value
            else:
                csend[g, step] = value.astype(jnp.bfloat16)
                pltpu.make_async_remote_copy(
                    src_ref=csend.at[g, step],
                    dst_ref=crecv.at[g, step],
                    send_sem=core_send.at[g],
                    recv_sem=core_recv.at[g],
                    device_id=sibling,
                    device_id_type=MESH,
                ).start()

    def store_z2(i, k, value):
        z2[k, i * COLS : (i + 1) * COLS, :] = value

    conv_own(hid, fband, store_z2)
    weight_grad(z2, cext[2 : 2 + ROWS, HALO : HALO + COLS, :].reshape(ROWS * COLS, CH), part2, 0)
    await_bytes(cext.at[pl.ds(0, 4)], halo_recv.at[1])
    backward(outer)
    weight_grad(z1own, gown[...], part1, 1)

    parts = (part2, part1)
    own_half = 2 * core

    def place_of(q):
        offset = (q - z + nz + zh) % nz - zh
        ahead = (offset > 0).astype(jnp.int32)
        behind = (offset < 0).astype(jnp.int32)
        far = (offset == -zh).astype(jnp.int32)
        return 2 * offset * (ahead - behind) - ahead - far

    places = [place_of(q) for q in range(nz)]

    def plane_chunk(p, store):
        row = (p // 2) * xr
        k, row = row // CH, pl.multiple_of(row % CH, xr)
        lanes = pl.ds(pl.multiple_of((p % 2) * 128, 128), 128)
        for g in range(2):
            rows = pl.ds(row, xr)
            total = parts[g][own_half + k, rows, lanes] + crecv[g, k, rows, lanes].astype(jnp.float32)
            for i in range(zh):
                store(places[g * zh + i], total[i * zr : (i + 1) * zr, :])

    def plane_send(slot, group):
        first, count = groups[group]
        some = pl.ds(first, count)
        pltpu.make_async_remote_copy(
            src_ref=xsend.at[slot, some],
            dst_ref=xrecv.at[slot, some],
            send_sem=x_send.at[group],
            recv_sem=x_recv.at[group],
            device_id=in_plane(plane_place(plane[slot])),
            device_id_type=MESH,
        ).start()

    def plane_scatter():
        for g in range(2):
            await_bytes(crecv.at[g], core_recv.at[g])
        for slot, step in enumerate(plane):

            def store(place, value, slot=slot):
                xsend[slot, place] = value.astype(jnp.bfloat16)

            plane_chunk(plane_place(step), store)
            plane_send(slot, len(groups) - 1)
        for group in (1, 0):
            for slot in range(len(plane)):
                plane_send(slot, group)

        def keep(place, value):
            xown[place] = value

        plane_chunk(me, keep)

    def z_scatter(group):
        first, count = groups[group]
        await_bytes(xrecv.at[:, pl.ds(first, count)], x_recv.at[group])
        terms = [xown[pl.ds(first, count)]]
        terms += [xrecv[s, pl.ds(first, count)].astype(jnp.float32) for s in range(len(plane))]
        zsend[pl.ds(first, count)] = tree_sum(terms)
        for place in reversed(range(first, first + count)):
            if place > 0:
                pltpu.make_async_remote_copy(
                    src_ref=zsend.at[place],
                    dst_ref=zrecv.at[place - 1],
                    send_sem=z_send.at[0],
                    recv_sem=z_recv.at[0],
                    device_id=in_z((z + nz + offsets[place]) % nz),
                    device_id_type=MESH,
                ).start()

    def z_gather():
        await_bytes(zrecv, z_recv.at[0])
        total = tree_sum([zsend[0]] + [zrecv[place] for place in range(nz - 1)])
        out[core, me, 0] = total.astype(jnp.bfloat16)
        for place in reversed(range(1, nz)):
            there = offsets.index(-offsets[place]) if 2 * offsets[place] < nz else place
            group = sum(there >= first for first, _ in last_groups) - 1
            pltpu.make_async_remote_copy(
                src_ref=out.at[core, me, 0],
                dst_ref=out.at[core, me, there],
                send_sem=zg_send.at[0],
                recv_sem=zg_recv.at[group],
                device_id=in_z((z + nz + offsets[place]) % nz),
                device_id_type=MESH,
            ).start()

    def gather(src, device, send, recv):
        pltpu.make_async_remote_copy(
            src_ref=src,
            dst_ref=src,
            send_sem=send,
            recv_sem=recv,
            device_id=device,
            device_id_type=MESH,
        ).start()

    def plane_gather(group):
        first, count = last_groups[group]
        own_chunk = 1 if first == 0 else 0
        if count > own_chunk:
            arrived = out.at[core, me, pl.ds(first + own_chunk, count - own_chunk)]
            await_bytes(arrived, zg_recv.at[group])
        some = out.at[core, me, pl.ds(first, count)]
        for step in plane:
            q = plane_place(step)
            gather(some, in_plane(q), xg_send.at[group], xg_recv.at[group])
            if group == 2:
                gather(some, in_plane(q, 1 - core), f_send.at[group], f_recv.at[group])
        if group == 2:
            gather(some, sibling, f_send.at[group], f_recv.at[group])

    def of_group(half, group, chips):
        first, count = last_groups[group]
        return out.at[half, pl.ds(0, chips), pl.ds(first, count)]

    q_of = [(z + nz + offset) % nz for offset in offsets]
    grad_of = [q // zh for q in q_of]
    row_of = [pl.multiple_of((q % zh) * zr, zr) for q in q_of]

    def emit(half, group):
        first, count = last_groups[group]
        for p in range(npl):
            k, base = (p // 2) * xr // CH, (p // 2) * xr % CH
            lanes = slice((p % 2) * 128, (p % 2 + 1) * 128)
            for place in range(first, first + count):
                rows = pl.ds(base + row_of[place], zr)
                sums_ref[grad_of[place], 2 * half + k, rows, lanes] = out[half, p, place].astype(
                    jnp.float32
                )

    def core_gather(group):
        await_bytes(of_group(core, group, npl - 1), xg_recv.at[group])
        if group < 2:
            gather(of_group(core, group, npl), sibling, f_send.at[group], f_recv.at[group])
        emit(core, group)

    def finish(group):
        await_bytes(of_group(core, group, npl), f_recv.at[group])
        emit(1 - core, group)

    plane_scatter()

    def store_back(i, k, value):
        zbuf[i * COLS : (i + 1) * COLS, k * CH : (k + 1) * CH] = value

    conv_own(gact, aband, store_back)
    gin_ref[...] = mix_back(zbuf[: ROWS * COLS, :], w1)

    z_await(2)
    for group in reversed(range(len(groups))):
        z_scatter(group)
    z_gather()
    for group in range(3):
        plane_gather(group)
    core_gather(0)
    core_gather(1)
    finish(0)
    finish(1)
    for which, ext in enumerate((gext, cext)):
        await_bytes(ext.at[pl.ds(0, 4)], halo_send.at[which])
        await_bytes(ext.at[pl.ds(0, ROWS), pl.ds(0, 2 * HALO)], halo_send.at[which + 2])
    for g in range(2):
        await_bytes(crecv.at[g], core_send.at[g])
    await_bytes(zrecv, z_send.at[0])
    await_bytes(out.at[core, me, pl.ds(0, nz - 1)], zg_send.at[0])
    for group, (first, count) in enumerate(groups):
        await_bytes(xrecv.at[:, pl.ds(first, count)], x_send.at[group])
    for group in range(2):
        await_bytes(of_group(core, group, npl - 1), xg_send.at[group])
        await_bytes(of_group(core, group, npl), f_send.at[group])
    core_gather(2)
    finish(2)
    await_bytes(of_group(core, 2, npl - 1), xg_send.at[2])
    await_bytes(of_group(core, 2, npl), f_send.at[2])


def write_out(g_ref, sums_ref, g_out, one_out, two_out, g_sem, sem):
    copies = [pltpu.make_async_copy(g_ref, g_out, g_sem)]
    for n, out in enumerate((two_out, one_out)):
        for k in range(KB):
            copies.append(pltpu.make_async_copy(sums_ref.at[n, k], out.at[k], sem.at[n, k]))
    for copy in copies:
        copy.start()
    for copy in copies:
        copy.wait()


def local(grid_in, basis, widths, weight_one, weight_two, cotangent):
    nlat, nlon = lax.axis_size("lat"), lax.axis_size("lon")
    npl, nz = nlat, nlon // 2
    zr = 4 * HALF // (npl * nz)
    bf16, f32 = jnp.bfloat16, jnp.float32
    vmem, dma = pltpu.VMEM, pltpu.SemaphoreType.DMA
    hbm = pl.BlockSpec(memory_space=pltpu.HBM)
    on_chip = pl.BlockSpec(memory_space=pltpu.VMEM)
    nlat_all = basis.shape[0]
    basis = basis.transpose(1, 2, 3, 0).reshape(3 * SPAN, KB, nlat_all)
    grid_in, weight_one, weight_two, cotangent = (
        pltpu.with_memory_space_constraint(x, pltpu.HBM)
        for x in (grid_in, weight_one, weight_two, cotangent)
    )
    basis, widths = (
        pltpu.with_memory_space_constraint(x, pltpu.HBM)
        for x in (basis, widths.reshape(1, nlat_all))
    )
    grad_in, sums = pl.pallas_call(
        functools.partial(kernel, nlat, nlon),
        out_shape=(
            jax.ShapeDtypeStruct((ROWS * COLS, CH), f32),
            jax.ShapeDtypeStruct((2, KB, CH, CH), f32),
        ),
        in_specs=[hbm] * 6,
        out_specs=(on_chip, on_chip),
        scratch_shapes=[
            vmem((XR, XC, CH), bf16),
            vmem((XR, XC, CH), bf16),
            vmem((3 * SPAN, KB, nlat_all), bf16),
            vmem((1, nlat_all), jnp.int32),
            vmem((2, KB * TAPS, nlat_all), f32),
            vmem((2, KB * SLOT, 4 * XC), f32),
            vmem((MR, KB * MC, 256), bf16),
            vmem((MR, KB * MC, 256), bf16),
            vmem((KB, CH, CH), bf16),
            vmem((KB, CH, CH), bf16),
            vmem((MR * MC, KB * CH), bf16),
            vmem((KB, ROWS * COLS, CH), bf16),
            vmem((KB, ROWS * COLS, CH), bf16),
            vmem((MR * MC, CH), f32),
            vmem((MR, XC, CH), bf16),
            vmem((MR, XC, CH), bf16),
            vmem((ROWS * COLS, CH), bf16),
            vmem((KB, CH, CH), f32),
            vmem((KB, CH, CH), f32),
            vmem((2, 2, CH, CH), bf16),
            vmem((2, 2, CH, CH), bf16),
            vmem((npl - 1, nz, zr, 128), bf16),
            vmem((npl - 1, nz, zr, 128), bf16),
            vmem((nz, zr, 128), f32),
            vmem((nz, zr, 128), f32),
            vmem((nz - 1, zr, 128), f32),
            vmem((2, npl, nz, zr, 128), bf16),
            dma((6,)),
        ]
        + [dma((4,))] * 2
        + [dma((2,))] * 2
        + [dma((3,))] * 10
        + [pltpu.SemaphoreType.REGULAR((3,))],
        compiler_params=pltpu.CompilerParams(
            collective_id=0, has_side_effects=True, vmem_limit_bytes=48 * 1024 * 1024
        ),
    )(grid_in, basis, widths, weight_one, weight_two, cotangent)
    wide = jax.ShapeDtypeStruct(weight_one.shape, f32)
    grad_in, one, two = pl.pallas_call(
        write_out,
        out_shape=(jax.ShapeDtypeStruct((ROWS * COLS, CH), f32), wide, wide),
        in_specs=[on_chip] * 2,
        out_specs=(hbm, hbm, hbm),
        scratch_shapes=[dma, dma((2, KB))],
        compiler_params=pltpu.CompilerParams(vmem_limit_bytes=16 * 1024 * 1024),
    )(grad_in, sums)
    return grad_in.reshape(grid_in.shape), one, two


def solution(mesh):
    placed = (P("lat", "lon", None), P(), P(), P(), P(), P("lat", "lon", None))
    return jax.shard_map(
        local,
        mesh=mesh,
        in_specs=placed,
        out_specs=(P("lat", "lon", None), P(), P()),
        check_vma=False,
    )
```
